512 devices in a mesh: elem: 32 (over z_lo, x), mode: 16 (over z_hi, y, core).
Axes of the slice: x: 4, y: 4, z: 16 (z_hi: 2, z_lo: 8; z = z_hi * 8 + z_lo), core: 2. Of those that a mesh axis runs over, the one named last changes fastest.
Arguments:
- displacement: float32 [2, 3, 512, 18432], P(None, None, 'mode', 'elem'), may hold values from -0.01171875 to 0.01171875
- metric: float32 [4, 18432], P(None, 'elem'), may hold values from -4 to 4
- weight_jac: float32 [18432], P('elem'), may hold values from 0.2 to 2
- radius: float32 [18432], P('elem'), may hold values from 0.5 to 2
- moduli: float32 [2, 512], P(None, 'elem'), may hold values from 0.5 to 4
- neighbours: int32 [512, 2], P('elem'), may hold values from -1 to 511, as said below
- inner_side: int32 [512], P('elem'), may hold values 0 or 1
- pressure: float32 [512], P('mode'), may hold values from -0.3 to 0.3
Outputs:
- residual: float32 [2, 3, 512, 18432], P(None, None, 'mode', 'elem')
The draws below stay inside these ranges and needn't reach their ends.
Inputs may be any that keep to these rules, and one draw needn't show every extreme that they name: The elements form one chain. neighbours[e, 0] is the element across the eta = -1 face of e and neighbours[e, 1] the element across its eta = +1 face, -1 at the chain's two ends; node (a, 0) of an element meets node (a, 5) of the element before it. The 16 elements of each index of elem form one run of the chain, stored in any order, and the runs follow the indices of elem in order.
All inputs are finite; a program needn't handle non-finite values. No bound on the sum of `inner_side` on one device may be relied on, other than what follows from the above.
Results may differ from the reference program's by a relative error of at most 0.00015.
Values sent between devices are 32-bit elements; how exact they have to be, the bound alone decides.
A program may use at most 64 MiB of HBM per device.

```python
import math
import jax
import jax.numpy as jnp
import numpy as np
from jax import lax

MODES = 256
ANGLES = 512
COEFS = 512
STATES = 2
EL_DEV = 16
ELEMS = 512
POINTS = 18432


def draw_displacement(key, part):
    key = jax.random.fold_in(key, 5)
    full_shape = (STATES, 3, COEFS, POINTS)
    slots = jnp.arange(COEFS, dtype=jnp.int32)
    orders = jnp.where(slots == 1, MODES, slots // 2).astype(jnp.float32)
    amplitude = 0.75 / MODES / (1.0 + orders)
    sample = jnp.clip(jax.random.normal(key, full_shape, jnp.float32), -4.0, 4.0)
    return sample * amplitude[:, None]


def draw_neighbours(key, part):
    key = jax.random.fold_in(key, 11)
    blocks = ELEMS // EL_DEV
    block_keys = jax.random.split(key, blocks)
    orders = jax.vmap(lambda k: jax.random.permutation(k, EL_DEV))(block_keys).astype(jnp.int32)
    starts = jnp.arange(blocks, dtype=jnp.int32) * EL_DEV
    chain_ids = (orders + starts[:, None]).reshape(-1)
    chain_ends = jnp.full((1,), -1, jnp.int32)
    prev_ids = jnp.concatenate([chain_ends, chain_ids[:-1]])
    next_ids = jnp.concatenate([chain_ids[1:], chain_ends])
    adjacency = jnp.zeros((ELEMS, 2), jnp.int32)
    adjacency = adjacency.at[chain_ids, 0].set(prev_ids).at[chain_ids, 1].set(next_ids)
    return adjacency


def set_ends(drawn, rng, low, top_value):
    place = [jax.random.randint(jax.random.fold_in(rng, axis), (), 0, length) for axis, length in enumerate(drawn.shape)]
    widest = drawn.shape.index(max(drawn.shape))
    beside = place[:widest] + [(place[widest] + 1) % drawn.shape[widest]] + place[widest + 1:]
    return drawn.at[tuple(place)].set(low).at[tuple(beside)].set(top_value)


def block_levels(own_key, extent, cuts, least, high):
    level = 1.0
    for dim, blocks in cuts:
        draws = jax.random.uniform(jax.random.fold_in(jax.random.fold_in(own_key, 6), dim), (blocks,), jnp.float32, least / len(cuts), high / len(cuts))
        level = level * jnp.repeat(jnp.exp(draws), extent[dim] // blocks).reshape((-1,) + (1,) * (len(extent) - 1 - dim))
    return level


def bell_draw(key, extent, scale, reach, cuts=(), kind=jnp.bfloat16):
    gain = block_levels(key, extent, cuts, -0.22, 0.18) if cuts else 1.0
    result = jax.random.normal(key, extent, jnp.float32) * scale * gain
    return jnp.minimum(jnp.maximum(result, -reach), reach).astype(kind)


def setup_inputs(seed: int = 0) -> dict:
    seeds = jax.random.split(jax.random.key(seed), 9)
    return {
        "displacement": draw_displacement(jax.random.fold_in(seeds[8], 71), 0),
        "metric": bell_draw(seeds[1], (4, POINTS), 1.0, 4.0, ((1, 32),), jnp.float32),
        "weight_jac": jnp.clip(jnp.exp(math.log(2.0) - 2.3025851 * jax.random.uniform(seeds[2], (POINTS,), jnp.float32) ** block_levels(seeds[2], (POINTS,), ((0, 32),), -0.2, 0.2)), 0.2, 2.0),
        "radius": jnp.clip(0.5 + 1.5 * jax.random.uniform(seeds[3], (POINTS,), jnp.float32) ** block_levels(seeds[3], (POINTS,), ((0, 32),), -0.2, 0.2), 0.5, 2.0),
        "moduli": jnp.clip(jnp.exp(math.log(4.0) - 2.0794415 * jax.random.uniform(seeds[4], (2, ELEMS), jnp.float32) ** block_levels(seeds[4], (2, ELEMS), ((1, 32),), -0.2, 0.2)), 0.5, 4.0),
        "neighbours": draw_neighbours(jax.random.fold_in(seeds[8], 71), 0),
        "inner_side": set_ends((jax.random.randint(seeds[6], (ELEMS,), 0, 2) < 1).astype(jnp.int32), jax.random.fold_in(seeds[6], 1), 0, 1),
        "pressure": bell_draw(seeds[7], (COEFS,), 0.05, 0.3, ((0, 16),), jnp.float32),
    }


precise = lax.Precision.HIGHEST

def line_derivative():
    inner_node = math.sqrt(1.0 / 3.0 - 2.0 * math.sqrt(7.0) / 21.0)
    outer_node = math.sqrt(1.0 / 3.0 + 2.0 * math.sqrt(7.0) / 21.0)
    gll_nodes = np.array([-1.0, -outer_node, -inner_node, inner_node, outer_node, 1.0])
    weights = np.array([1.0 / np.prod([gll_nodes[j] - gll_nodes[k] for k in range(6) if k != j]) for j in range(6)])
    derivative = np.zeros((6, 6))
    for i in range(6):
        for j in range(6):
            if i != j:
                derivative[i, j] = weights[j] / weights[i] / (gll_nodes[i] - gll_nodes[j])
        derivative[i, i] = -np.sum(derivative[i])
    return derivative

def node_tables():
    derivative = line_derivative()
    identity = np.eye(6)
    along_xi = np.kron(derivative, identity)
    along_eta = np.kron(identity, derivative)
    return (jnp.asarray(along_xi, jnp.float32), jnp.asarray(along_eta, jnp.float32))

def apply_rows(values, matrix):
    span_width = matrix.shape[0]
    leading = values.shape[:-1]
    blocks = values.reshape(leading + (values.shape[-1] // span_width, span_width))
    return jnp.matmul(blocks, matrix.T, precision=precise).reshape(values.shape)

def apply_cols(values, matrix):
    span_width = matrix.shape[0]
    leading = values.shape[:-1]
    blocks = values.reshape(leading + (values.shape[-1] // span_width, span_width))
    return jnp.matmul(blocks, matrix, precision=precise).reshape(values.shape)

def rotate(values, orders):
    full_shape = values.shape
    paired = values.reshape(full_shape[:-2] + (full_shape[-2] // 2, 2, full_shape[-1]))
    weights = orders[:, None]
    turned = jnp.stack([weights * paired[..., 1, :], -weights * paired[..., 0, :]], axis=-2)
    return turned.reshape(full_shape)

def gradient_fields(displaced, geometry, orders, xi_table, eta_table):
    along_xi = apply_rows(displaced, xi_table)
    along_eta = apply_rows(displaced, eta_table)
    radial = geometry[0] * along_xi + geometry[2] * along_eta
    axial_part = geometry[1] * along_xi + geometry[3] * along_eta
    turned = rotate(displaced, orders)
    hoop_part = jnp.stack([turned[..., 0, :, :] - displaced[..., 1, :, :], turned[..., 1, :, :] + displaced[..., 0, :, :], turned[..., 2, :, :]], axis=-3)
    return jnp.concatenate([radial, axial_part, hoop_part], axis=-3)

def stress(angular, radius_part, shear_part, bulk_part):
    inverse_r = 1.0 / radius_part
    pieces = [angular[..., i, :, :] for i in range(9)]
    deform = [[1.0 + pieces[0], inverse_r * pieces[6], pieces[3]], [pieces[1], 1.0 + inverse_r * pieces[7], pieces[4]], [pieces[2], inverse_r * pieces[8], 1.0 + pieces[5]]]
    cofactor = [[deform[(i + 1) % 3][(j + 1) % 3] * deform[(i + 2) % 3][(j + 2) % 3] - deform[(i + 1) % 3][(j + 2) % 3] * deform[(i + 2) % 3][(j + 1) % 3] for j in range(3)] for i in range(3)]
    volume = deform[0][0] * cofactor[0][0] + deform[0][1] * cofactor[0][1] + deform[0][2] * cofactor[0][2]
    factor = bulk_part * (volume - 1.0) - shear_part
    first_piola = [[shear_part * deform[i][j] + factor * cofactor[i][j] for j in range(3)] for i in range(3)]
    return jnp.stack([radius_part * first_piola[0][0], radius_part * first_piola[1][0], radius_part * first_piola[2][0], radius_part * first_piola[0][2], radius_part * first_piola[1][2], radius_part * first_piola[2][2], first_piola[0][1], first_piola[1][1], first_piola[2][1]], axis=-3)

def divergence(projected, geometry, weight_part, orders, xi_table, eta_table):
    radial = projected[..., 0:3, :, :]
    axial_part = projected[..., 3:6, :, :]
    along_xi = weight_part * (geometry[0] * radial + geometry[1] * axial_part)
    along_eta = weight_part * (geometry[2] * radial + geometry[3] * axial_part)
    spread = apply_cols(along_xi, xi_table) + apply_cols(along_eta, eta_table)
    shear_rt = projected[..., 6, :, :]
    shear_tt = projected[..., 7, :, :]
    shear_zt = projected[..., 8, :, :]
    hoop_part = jnp.stack([shear_tt - rotate(shear_rt, orders), -rotate(shear_tt, orders) - shear_rt, -rotate(shear_zt, orders)], axis=-3)
    return spread + weight_part * hoop_part

def angle_basis():
    counts = jnp.arange(ANGLES, dtype=jnp.int32)
    orders = jnp.arange(MODES, dtype=jnp.int32)
    phases = (counts[:, None] * orders[None, :] % ANGLES).astype(jnp.float32) * (2.0 * math.pi / ANGLES)
    nyquist = jnp.where(counts % 2 == 0, 1.0, -1.0).astype(jnp.float32)
    sines = jnp.sin(phases).at[:, 0].set(nyquist)
    return jnp.stack([jnp.cos(phases), sines], axis=-1).reshape(ANGLES, 2 * MODES)

def reference(displacement, metric, weight_jac, radius, moduli, neighbours, inner_side, pressure):
    blocks = ELEMS // EL_DEV
    block_points = EL_DEV * 36
    angle_table = angle_basis()
    angle_step = 2.0 * math.pi / ANGLES
    orders = jnp.arange(MODES, dtype=jnp.float32)
    xi_table, eta_table = node_tables()
    shear_all = jnp.repeat(moduli[0], 36)
    bulk_all = jnp.repeat(moduli[1], 36)

    def one_block(inputs):
        moved, geometry, weight_part, radius_part, shear_part, bulk_part = inputs
        gradients = gradient_fields(moved, geometry, orders, xi_table, eta_table)
        angular = jnp.einsum('sfcp,kc->sfkp', gradients, angle_table, precision=precise)
        stress_terms = stress(angular, radius_part, shear_part, bulk_part)
        projected = jnp.einsum('sfkp,kc->sfcp', stress_terms, angle_table, precision=precise) * angle_step
        return divergence(projected, geometry, weight_part, orders, xi_table, eta_table)
    per_block = (jnp.moveaxis(displacement.reshape(STATES, 3, COEFS, blocks, block_points), 3, 0), jnp.moveaxis(metric.reshape(4, blocks, block_points), 1, 0), weight_jac.reshape(blocks, block_points), radius.reshape(blocks, block_points), shear_all.reshape(blocks, block_points), bulk_all.reshape(blocks, block_points))
    volume = jnp.moveaxis(lax.map(one_block, per_block), 0, 3).reshape(STATES, 3, COEFS, POINTS)
    node_index = jnp.arange(POINTS, dtype=jnp.int32) % 36
    xi_pos = node_index // 6
    eta_pos = node_index % 6
    face_side = jnp.repeat(inner_side, 36)
    on_face = xi_pos == 5 * face_side
    outward = (2 * face_side - 1).astype(jnp.float32)
    face_weight = jnp.where(on_face, 15.0 * outward * weight_jac * radius, 0.0)
    load_term = pressure[:, None] * face_weight[None, :]
    loaded = volume + jnp.stack([load_term * metric[0], jnp.zeros_like(load_term), load_term * metric[1]], axis=0)
    prev_elem = jnp.repeat(neighbours[:, 0], 36)
    next_elem = jnp.repeat(neighbours[:, 1], 36)
    lower_face = eta_pos == 0
    upper_face = eta_pos == 5
    partner = jnp.where(lower_face, prev_elem * 36 + xi_pos * 6 + 5, next_elem * 36 + xi_pos * 6)
    linked = jnp.where(lower_face, prev_elem >= 0, upper_face & (next_elem >= 0))
    partner = jnp.where(linked, partner, 0).astype(jnp.int32)
    return loaded + jnp.where(linked, jnp.take(loaded, partner, axis=3), 0.0)
```

```python
import math

import jax
import jax.numpy as jnp
import ml_dtypes
import numpy as np
from jax import lax
from jax.experimental import pallas as pl
from jax.experimental.pallas import tpu as pltpu
from jax.sharding import PartitionSpec as P

MODES = 256
ANGLES = 512
COEFS = 512
NODES = 36
PEERS = 16
OWN = 32
POINTS = 576
WIDE = 640
BLOCK = 128
MESH = pl.DeviceIdType.MESH
f32, bf16 = jnp.float32, jnp.bfloat16

OFFSETS = [(dz, dy, dc) for dz in (1, 0) for dy in (2, 1, 3, 0) for dc in (1, 0) if dz + dy + dc]


def line_derivative():
    inner_node = math.sqrt(1.0 / 3.0 - 2.0 * math.sqrt(7.0) / 21.0)
    outer_node = math.sqrt(1.0 / 3.0 + 2.0 * math.sqrt(7.0) / 21.0)
    gll_nodes = np.array([-1.0, -outer_node, -inner_node, inner_node, outer_node, 1.0])
    weights = np.array(
        [1.0 / np.prod([gll_nodes[j] - gll_nodes[k] for k in range(6) if k != j]) for j in range(6)]
    )
    derivative = np.zeros((6, 6))
    for i in range(6):
        for j in range(6):
            if i != j:
                derivative[i, j] = weights[j] / weights[i] / (gll_nodes[i] - gll_nodes[j])
        derivative[i, i] = -np.sum(derivative[i])
    return derivative


def halves(table):
    high = table.astype(np.float32).astype(ml_dtypes.bfloat16)
    low = (table - high.astype(np.float64)).astype(np.float32).astype(ml_dtypes.bfloat16)
    return high, low


def tables():
    counts = np.arange(ANGLES)
    orders = np.arange(MODES)
    phases = (counts[:, None] * orders[None, :] % ANGLES) * (2.0 * math.pi / ANGLES)
    basis = np.zeros((ANGLES, COEFS))
    basis[:, 0::2] = np.cos(phases)
    basis[:, 1::2] = np.sin(phases)
    basis[:, 1] = np.where(counts % 2 == 0, 1.0, -1.0)
    turned = np.zeros((ANGLES, COEFS))
    turned[:, 1::2] = orders * basis[:, 0::2]
    turned[:, 0::2] = -orders * basis[:, 1::2]
    both = np.concatenate([basis, turned], axis=0)
    forward = halves(both)
    backward = halves(both.T * (2.0 * math.pi / ANGLES))
    derivative = line_derivative()
    along_xi = np.kron(derivative, np.eye(6))
    along_eta = np.kron(np.eye(6), derivative)
    spread = np.zeros((128, 768))
    for c in range(3):
        rows = slice(NODES * c, NODES * c + NODES)
        spread[rows, 128 * c : 128 * c + NODES] = along_xi.T
        spread[rows, 384 + 128 * c : 384 + 128 * c + NODES] = along_eta.T
    lanes = np.full((8, WIDE), -1, np.int32)
    points = np.arange(POINTS)
    lanes[0, :POINTS] = points // NODES
    lanes[1, :POINTS] = points % NODES // 6
    lanes[2, :POINTS] = points % 6
    lanes[3, :72] = np.arange(72) % 6
    lanes[4, :72] = np.arange(72) // 6
    return forward, backward, halves(spread), halves(spread.T), lanes


def split(values):
    high = values.astype(bf16)
    return high, (values - high.astype(f32)).astype(bf16)


def dot(a, b):
    return jnp.dot(a, b, preferred_element_type=f32)


def turn(values, shift):
    shift = shift % 128
    return pltpu.roll(values, shift, 1) if shift else values


def kernel(
    disp, geo, pres, lanes, neigh, side, moduli,
    fwd_hi, fwd_lo, bwd_hi, bwd_lo, der_hi, der_lo, ted_hi, ted_lo,
    out,
    pack, got1, got2, state1, fields, back0, back1, home0, home1, perm, rims, rim_out, rim_in, base,
    tfh, tfl, tbh, tbl, tdh, tdl, teh, tel,
    table_sem, send1, recv1, send2, recv2, send3, recv3, send4, recv4, rim_send, rim_recv,
):
    elem = lax.axis_index("elem")
    mode = lax.axis_index("mode")
    runs = lax.axis_size("elem")
    half, rest = mode // 8, mode % 8
    row, core = rest // 2, rest % 2

    def peer(dz, dy, dc):
        return (half + dz + 2) % 2 * 8 + (row + dy + 4) % 4 * 2 + (core + dc + 2) % 2

    barrier = pltpu.get_barrier_semaphore()
    for dz, dy, dc in OFFSETS:
        pl.semaphore_signal(barrier, inc=1, device_id=(elem, peer(-dz, -dy, -dc)), device_id_type=MESH)

    @pl.when(elem > 0)
    def _():
        pl.semaphore_signal(barrier, inc=1, device_id=(elem - 1, mode), device_id_type=MESH)

    @pl.when(elem < runs - 1)
    def _():
        pl.semaphore_signal(barrier, inc=1, device_id=(elem + 1, mode), device_id_type=MESH)

    table_copies = []
    for i, (src, dst) in enumerate(
        [(fwd_hi, tfh), (fwd_lo, tfl), (der_hi, tdh), (der_lo, tdl), (ted_hi, teh), (ted_lo, tel),
         (bwd_hi, tbh), (bwd_lo, tbl)]
    ):
        copy = pltpu.make_async_copy(src, dst, table_sem.at[i])
        copy.start()
        table_copies.append(copy)

    lane = lax.broadcasted_iota(jnp.int32, (OWN, 128), 1)
    lane8 = lax.broadcasted_iota(jnp.int32, (8, 128), 1)

    def column(s, c, g):
        if g < 4:
            return disp[s, c, :, 128 * g : 128 * g + 128]
        return jnp.concatenate([disp[s, c, :, 512:576], jnp.zeros((OWN, 64), f32)], axis=1)

    def gather_element(s, j, base_lane):
        result = jnp.zeros((OWN, 128), f32)
        for c in range(3):
            target = NODES * c + base_lane
            first = NODES * j
            for g in range(first // 128, (first + NODES - 1) // 128 + 1):
                low = max(first, 128 * g)
                high = min(first + NODES, 128 * g + 128)
                moved = turn(column(s, c, g), target - (first - 128 * g))
                begin = (target + low - first) % 128
                end = begin + high - low
                inside = (lane >= begin) & (lane < end)
                if end > 128:
                    inside = (lane >= begin) | (lane < end - 128)
                result = jnp.where(inside, moved, result)
        return result

    def pack_rows(full, ragged):
        last = ragged[24:32]
        tails = [turn(last, 88), turn(last, 48), turn(last, 8)]
        rows = [jnp.where(lane8 < 88, ragged[8 * t : 8 * t + 8], tails[t]) for t in range(3)]
        return jnp.where(lane < 108, full, ragged), jnp.concatenate(rows, axis=0)

    def unpack_ragged(first, second):
        rows = [
            jnp.where(lane8 < 88, second[8 * t : 8 * t + 8], first[8 * t : 8 * t + 8]) for t in range(3)
        ]
        moved = [turn(second[0:8], -88), turn(second[8:16], -48), turn(second[16:24], -8)]
        last = jnp.where(lane8 < 40, moved[0], jnp.where(lane8 < 80, moved[1], moved[2]))
        rows.append(jnp.where(lane8 < 88, last, first[24:32]))
        return jnp.concatenate(rows, axis=0)

    for j in range(PEERS):
        full = gather_element(0, j, 0)
        ragged = gather_element(1, j, 108)
        top, bottom = pack_rows(full, ragged)
        pack[j, 0:32, :] = top
        pack[j, 32:56, :] = bottom

    neighbours_there = 2 - (elem == 0).astype(jnp.int32) - (elem == runs - 1).astype(jnp.int32)
    pl.semaphore_wait(barrier, len(OFFSETS) + neighbours_there)

    def exchange(source, target, send, recv):
        copies = []
        for i, (dz, dy, dc) in enumerate(OFFSETS):
            to = peer(dz, dy, dc)
            copy = pltpu.make_async_remote_copy(
                src_ref=source(to),
                dst_ref=target.at[mode],
                send_sem=send.at[i],
                recv_sem=recv.at[i],
                device_id=(elem, to),
                device_id_type=MESH,
            )
            copy.start()
            copies.append(copy)
        return copies

    there1 = exchange(lambda to: pack.at[to, 0:32], got1, send1, recv1)
    there2 = exchange(lambda to: pack.at[to, 32:56], got2, send2, recv2)
    got1[mode] = pack[mode, 0:32, :]
    got2[mode] = pack[mode, 32:56, :]

    def own_row(i):
        moved = pltpu.roll(geo[...], (WIDE - NODES * mode) % WIDE, 1)
        return moved[i : i + 1, 0:128]

    lane1 = lax.broadcasted_iota(jnp.int32, (1, 128), 1)
    real = lane1 < NODES
    xi_r, xi_z, eta_r, eta_z, weight, radius = [jnp.where(real, own_row(i), 0.0) for i in range(6)]
    radius = jnp.where(real, radius, 1.0)
    rho = 1.0 / radius
    shear = moduli[0, mode]
    bulk = moduli[1, mode]
    scale = weight * radius
    back_rows = [scale * xi_r, scale * xi_z, scale * eta_r, scale * eta_z]

    first_elem = elem * PEERS
    head = jnp.int32(0)
    tail = jnp.int32(0)
    e_lane, a_lane, b_lane = lanes[0:1, :], lanes[1:2, :], lanes[2:3, :]
    partner = jnp.full((1, WIDE), -1, jnp.int32)
    sides = jnp.zeros((1, WIDE), jnp.int32)
    for e in range(PEERS):
        prev = neigh[e, 0] - first_elem
        nxt = neigh[e, 1] - first_elem
        prev_here = (prev >= 0) & (prev < PEERS)
        next_here = (nxt >= 0) & (nxt < PEERS)
        head = head + jnp.where(prev_here, 0, e)
        tail = tail + jnp.where(next_here, 0, e)
        low = jnp.where(prev_here, prev * NODES + 5, -10000)
        high = jnp.where(next_here, nxt * NODES, -10000)
        here = e_lane == e
        partner = jnp.where(here & (b_lane == 0), low + 6 * a_lane, partner)
        partner = jnp.where(here & (b_lane == 5), high + 6 * a_lane, partner)
        sides = jnp.where(here, side[e], sides)
    for g in range(5):
        rows = lax.broadcasted_iota(jnp.int32, (128, WIDE), 0) + 128 * g
        perm[128 * g : 128 * g + 128, :] = jnp.where(rows == partner, 1.0, 0.0).astype(bf16)
    node = lanes[3:4, 0:128]
    head_node = jnp.where(node >= 0, head * NODES + 6 * node, -1)
    tail_node = jnp.where(node >= 0, tail * NODES + 6 * node + 5, -1)
    for g in range(5):
        rows = lax.broadcasted_iota(jnp.int32, (128, 128), 0) + 128 * g
        rims[128 * g : 128 * g + 128, 0:128] = jnp.where(rows == head_node, 1.0, 0.0).astype(bf16)
        rims[128 * g : 128 * g + 128, 128:256] = jnp.where(rows == tail_node, 1.0, 0.0).astype(bf16)
    facing = (a_lane == 5 * sides) & (e_lane >= 0)
    outward = (2 * sides - 1).astype(f32)
    face = jnp.where(facing, 15.0 * outward * geo[4:5, :] * geo[5:6, :], 0.0)
    pressure = pres[...]
    base[0] = pressure * (face * geo[0:1, :])
    base[1] = pressure * (face * geo[1:2, :])

    for copy in table_copies:
        copy.wait()

    def evaluate(coefs, result_block):
        hi, lo = split(coefs)
        both = jnp.concatenate([hi, lo], axis=1)

        def to_angles(first):
            rows = pl.ds(pl.multiple_of(first, BLOCK), BLOCK)
            wide = dot(tfh[rows, :], both)
            return wide[:, 0:128] + wide[:, 128:256] + dot(tfl[rows, :], hi)

        def one_block(k, _):
            u = to_angles(k * BLOCK)
            r = to_angles(ANGLES + k * BLOCK)
            u_hi, u_lo = split(u)
            grads = dot(u_hi, tdh[...]) + dot(u_lo, tdh[...]) + dot(u_hi, tdl[...])
            v = [None] * 9
            for c in range(3):
                ax = grads[:, 128 * c : 128 * c + 128]
                ae = grads[:, 384 + 128 * c : 512 + 128 * c]
                v[c] = xi_r * ax + eta_r * ae
                v[3 + c] = xi_z * ax + eta_z * ae
            v[6] = r - turn(u, -NODES)
            v[7] = turn(r, -NODES) + u
            v[8] = turn(r, -2 * NODES)
            deform = [
                [1.0 + v[0], rho * v[6], v[3]],
                [v[1], 1.0 + rho * v[7], v[4]],
                [v[2], rho * v[8], 1.0 + v[5]],
            ]
            cof = [
                [
                    deform[(i + 1) % 3][(j + 1) % 3] * deform[(i + 2) % 3][(j + 2) % 3]
                    - deform[(i + 1) % 3][(j + 2) % 3] * deform[(i + 2) % 3][(j + 1) % 3]
                    for j in range(3)
                ]
                for i in range(3)
            ]
            volume = deform[0][0] * cof[0][0] + deform[0][1] * cof[0][1] + deform[0][2] * cof[0][2]
            factor = bulk * (volume - 1.0) - shear
            piola = [
                [shear * deform[i][j] + factor * cof[i][j] for j in range(3)] for i in range(3)
            ]
            parts = [back_rows[0] * piola[c][0] + back_rows[1] * piola[c][2] for c in range(3)]
            parts += [back_rows[2] * piola[c][0] + back_rows[3] * piola[c][2] for c in range(3)]
            p_hi, p_lo = split(jnp.concatenate(parts, axis=1))
            hoop = [weight * piola[c][1] for c in range(3)]
            straight = dot(p_hi, teh[...]) + dot(p_lo, teh[...]) + dot(p_hi, tel[...])
            straight = straight + hoop[1] - turn(hoop[0], NODES)
            turned = hoop[0] + turn(hoop[1], NODES) + turn(hoop[2], 2 * NODES)
            for start, value in ((0, straight), (ANGLES, turned)):
                v_hi, v_lo = split(value)
                rows = pl.ds(pl.multiple_of(start + k * BLOCK, BLOCK), BLOCK)
                fields[rows, 0:128] = v_hi
                fields[rows, 128:256] = v_lo
            return 0

        lax.fori_loop(0, ANGLES // BLOCK, one_block, 0)

        def back_block(k, _):
            rows = pl.ds(pl.multiple_of(k * BLOCK, BLOCK), BLOCK)
            wide = dot(tbh[rows, :], fields[...])
            result_block(k, wide[:, 0:128] + wide[:, 128:256] + dot(tbl[rows, :], fields[:, 0:128]))
            return 0

        lax.fori_loop(0, COEFS // BLOCK, back_block, 0)

    for copy in there1:
        copy.wait_recv()

    def keep_ragged(k, block):
        block = turn(block, 108)
        for q in range(BLOCK // OWN):
            _, bottom = pack_rows(block[OWN * q : OWN * q + OWN], block[OWN * q : OWN * q + OWN])
            back0[k * (BLOCK // OWN) + q] = bottom
            back1[k * (BLOCK // OWN) + q] = block[OWN * q : OWN * q + OWN]

    evaluate(got1[...].reshape(COEFS, 128), keep_ragged)
    again0 = exchange(lambda to: back0.at[to], home0, send3, recv3)
    home0[mode] = back0[mode]

    for copy in there2:
        copy.wait_recv()
    for i in range(PEERS):
        state1[OWN * i : OWN * i + OWN, :] = turn(unpack_ragged(got1[i], got2[i]), 20)

    def keep_full(k, block):
        for q in range(BLOCK // OWN):
            i = k * (BLOCK // OWN) + q
            back1[i] = jnp.where(lane < 108, block[OWN * q : OWN * q + OWN], back1[i])

    evaluate(state1[...], keep_full)
    again1 = exchange(lambda to: back1.at[to], home1, send4, recv4)
    home1[mode] = back1[mode]

    for copy in again0 + again1:
        copy.wait_recv()

    pieces = [[turn(unpack_ragged(home1[i], home0[i]), 20) for i in range(PEERS)],
              [home1[i] for i in range(PEERS)]]
    loaded = []
    for s in range(2):
        for c in range(3):
            columns = []
            for g in range(5):
                acc = jnp.zeros((OWN, 128), f32)
                for i in range(PEERS):
                    low = max(NODES * i, 128 * g) - 128 * g
                    high = min(NODES * i + NODES, 128 * g + 128) - 128 * g
                    if low < high:
                        moved = turn(pieces[s][i], NODES * i - 128 * g - NODES * c)
                        acc = jnp.where((lane >= low) & (lane < high), moved, acc)
                columns.append(acc)
            whole = jnp.concatenate(columns, axis=1)
            if c == 0:
                whole = whole + base[0]
            elif c == 2:
                whole = whole + base[1]
            loaded.append(whole)
    loaded = jnp.concatenate(loaded, axis=0)
    l_hi, l_lo = split(loaded)

    traces = dot(l_hi, rims[...]) + dot(l_lo, rims[...])
    slot = lanes[4:5, 0:128]
    for way in range(2):
        trace = traces[:, 128 * way : 128 * way + 128]
        for s in range(2):
            tile = jnp.zeros((8, 128), f32)
            for t in range(12):
                tile = jnp.where(slot == t, trace[96 * s + 8 * t : 96 * s + 8 * t + 8], tile)
            rim_out[way, 8 * s : 8 * s + 8, :] = tile

    to_prev = pltpu.make_async_remote_copy(
        src_ref=rim_out.at[0], dst_ref=rim_in.at[1], send_sem=rim_send.at[0], recv_sem=rim_recv.at[1],
        device_id=(jnp.maximum(elem - 1, 0), mode), device_id_type=MESH,
    )
    to_next = pltpu.make_async_remote_copy(
        src_ref=rim_out.at[1], dst_ref=rim_in.at[0], send_sem=rim_send.at[1], recv_sem=rim_recv.at[0],
        device_id=(jnp.minimum(elem + 1, runs - 1), mode), device_id_type=MESH,
    )

    @pl.when(elem > 0)
    def _():
        to_prev.start()

    @pl.when(elem < runs - 1)
    def _():
        to_next.start()

    result = loaded + dot(l_hi, perm[...]) + dot(l_lo, perm[...])

    @pl.when(elem > 0)
    def _():
        to_next.wait_recv()

    @pl.when(elem < runs - 1)
    def _():
        to_prev.wait_recv()

    arrived = []
    for way, there in ((0, elem > 0), (1, elem < runs - 1)):
        rows = []
        for s in range(2):
            tile = jnp.where(there, rim_in[way, 8 * s : 8 * s + 8, :], 0.0)
            rows += [jnp.where(slot == t, tile, 0.0) for t in range(12)]
        arrived.append(jnp.concatenate(rows, axis=0))
    a_hi, a_lo = split(jnp.concatenate(arrived, axis=1))
    for part in (a_hi, a_lo):
        result = result + lax.dot_general(
            part, rims[...], (((1,), (1,)), ((), ())), preferred_element_type=f32
        )
    for s in range(2):
        for c in range(3):
            first = 96 * s + 32 * c
            out[s, c] = result[first : first + 32, 0:POINTS]

    for copy in there1 + there2 + again0 + again1:
        copy.wait_send()

    @pl.when(elem > 0)
    def _():
        to_prev.wait_send()

    @pl.when(elem < runs - 1)
    def _():
        to_next.wait_send()


def on_device(displacement, metric, weight_jac, radius, moduli, neighbours, inner_side, pressure):
    forward, backward, spread, gather, lanes = tables()
    geo = jnp.concatenate(
        [metric, weight_jac[None, :], radius[None, :], jnp.zeros((2, POINTS), f32)], axis=0
    )
    geo = jnp.pad(geo, ((0, 0), (0, WIDE - POINTS)))
    vmem = pl.BlockSpec(memory_space=pltpu.VMEM)
    smem = pl.BlockSpec(memory_space=pltpu.SMEM)
    anywhere = pl.BlockSpec(memory_space=pl.ANY)
    constants = [jnp.asarray(t) for t in (*forward, *backward, *spread, *gather)]
    dma = pltpu.SemaphoreType.DMA((len(OFFSETS),))
    return pl.pallas_call(
        kernel,
        out_shape=jax.ShapeDtypeStruct((2, 3, OWN, POINTS), f32),
        in_specs=[vmem] * 4 + [smem] * 3 + [anywhere] * 8,
        out_specs=vmem,
        scratch_shapes=[
            pltpu.VMEM((PEERS, 56, 128), f32),
            pltpu.VMEM((PEERS, 32, 128), f32),
            pltpu.VMEM((PEERS, 24, 128), f32),
            pltpu.VMEM((COEFS, 128), f32),
            pltpu.VMEM((2 * ANGLES, 256), bf16),
            pltpu.VMEM((PEERS, 24, 128), f32),
            pltpu.VMEM((PEERS, 32, 128), f32),
            pltpu.VMEM((PEERS, 24, 128), f32),
            pltpu.VMEM((PEERS, 32, 128), f32),
            pltpu.VMEM((WIDE, WIDE), bf16),
            pltpu.VMEM((WIDE, 256), bf16),
            pltpu.VMEM((2, 16, 128), f32),
            pltpu.VMEM((2, 16, 128), f32),
            pltpu.VMEM((2, OWN, WIDE), f32),
            pltpu.VMEM((2 * ANGLES, COEFS), bf16),
            pltpu.VMEM((2 * ANGLES, COEFS), bf16),
            pltpu.VMEM((COEFS, 2 * ANGLES), bf16),
            pltpu.VMEM((COEFS, 2 * ANGLES), bf16),
            pltpu.VMEM((128, 768), bf16),
            pltpu.VMEM((128, 768), bf16),
            pltpu.VMEM((768, 128), bf16),
            pltpu.VMEM((768, 128), bf16),
            pltpu.SemaphoreType.DMA((8,)),
            dma, dma, dma, dma, dma, dma, dma, dma,
            pltpu.SemaphoreType.DMA((2,)),
            pltpu.SemaphoreType.DMA((2,)),
        ],
        compiler_params=pltpu.CompilerParams(
            collective_id=0, has_side_effects=True, vmem_limit_bytes=48 * 2**20
        ),
        name="bellows",
    )(
        displacement, geo, pressure[:, None], jnp.asarray(lanes), neighbours, inner_side, moduli,
        *constants,
    )


def solution(mesh):
    placed = (
        P(None, None, "mode", "elem"),
        P(None, "elem"),
        P("elem"),
        P("elem"),
        P(None, "elem"),
        P("elem", None),
        P("elem"),
        P("mode"),
    )
    return jax.shard_map(
        on_device,
        mesh=mesh,
        in_specs=placed,
        out_specs=P(None, None, "mode", "elem"),
        check_vma=False,
    )
```

```python
import math

import jax
import jax.numpy as jnp
import ml_dtypes
import numpy as np
from jax import lax
from jax.experimental import pallas as pl
from jax.experimental.pallas import tpu as pltpu
from jax.sharding import PartitionSpec as P

MODES = 256
ANGLES = 512
COEFS = 512
NODES = 36
PEERS = 16
OWN = 32
POINTS = 576
WIDE = 640
HALF = 272
STRIP = 16
MESH = pl.DeviceIdType.MESH
f32, bf16 = jnp.float32, jnp.bfloat16

LOCAL = [(dy, dc) for dy in (2, 1, 3, 0) for dc in (1, 0) if dy + dc]
CROSS = [(dy, dc, 1 - (dy + dc) % 2 * 2) for dy in (2, 1, 3, 0) for dc in (0, 1)]
LEG = 4


def line_derivative():
    inner_node = math.sqrt(1.0 / 3.0 - 2.0 * math.sqrt(7.0) / 21.0)
    outer_node = math.sqrt(1.0 / 3.0 + 2.0 * math.sqrt(7.0) / 21.0)
    gll_nodes = np.array([-1.0, -outer_node, -inner_node, inner_node, outer_node, 1.0])
    weights = np.array(
        [1.0 / np.prod([gll_nodes[j] - gll_nodes[k] for k in range(6) if k != j]) for j in range(6)]
    )
    derivative = np.zeros((6, 6))
    for i in range(6):
        for j in range(6):
            if i != j:
                derivative[i, j] = weights[j] / weights[i] / (gll_nodes[i] - gll_nodes[j])
        derivative[i, i] = -np.sum(derivative[i])
    return derivative


def halves(table):
    high = table.astype(np.float32).astype(ml_dtypes.bfloat16)
    low = (table - high.astype(np.float64)).astype(np.float32).astype(ml_dtypes.bfloat16)
    return high, low


def tables():
    counts = np.arange(HALF)
    orders = np.arange(MODES)
    phases = (counts[:, None] * orders[None, :] % ANGLES) * (2.0 * math.pi / ANGLES)
    used = (counts <= ANGLES // 2)[:, None]
    cosines, sines = np.cos(phases) * used, np.sin(phases) * used
    from_cos = np.concatenate([cosines, -orders * sines], axis=0)
    from_sin = np.concatenate([sines, orders * cosines], axis=0)
    step = 2.0 * math.pi / ANGLES
    ends = np.where(counts == 0, 0.5, 1.0)[: ANGLES // 2, None]
    cosines, sines = step * ends * cosines[: ANGLES // 2], step * sines[: ANGLES // 2]
    to_cos = np.concatenate([cosines, -orders * sines], axis=0).T
    to_sin = np.concatenate([sines, orders * cosines], axis=0).T
    derivative = line_derivative()
    slopes = [np.kron(derivative, np.eye(6)).T, np.kron(np.eye(6), derivative).T]
    spread = np.zeros((256, 768))
    for way, slope in enumerate(slopes):
        for c in range(3):
            column = 384 * way + 128 * c
            even, odd = NODES * c, 128 + NODES * c
            spread[even : even + NODES, column : column + 2 * NODES] = np.concatenate([slope, slope], axis=1)
            spread[odd : odd + NODES, column : column + 2 * NODES] = np.concatenate([slope, -slope], axis=1)
    blocks = [from_cos, from_sin, to_cos[:, 0:256], to_cos[:, 256:512], to_sin[:, 0:256], to_sin[:, 256:512]]
    blocks += [spread[:, 0:256], spread[:, 256:512], spread[:, 512:768], spread.T]
    return np.concatenate([part for block in blocks for part in halves(block)], axis=0)


BLOCK_ROWS = [2 * HALF] * 2 + [256] * 4 + [256] * 3 + [768]
BLOCK_START = np.concatenate([[0], np.cumsum([2 * n for n in BLOCK_ROWS])]).tolist()


def split(values):
    high = values.astype(bf16)
    return high, (values - high.astype(f32)).astype(bf16)


def dot(a, b):
    return jnp.dot(a, b, preferred_element_type=f32)


def turn(values, shift):
    shift = shift % 128
    return pltpu.roll(values, shift, 1) if shift else values


def evaluate(coefs, result, rows, shear, bulk, table, scratch):
    def block(i):
        first, count = BLOCK_START[i], BLOCK_ROWS[i]
        return table[first : first + count, :], table[first + count : first + 2 * count, :]

    even_odd, turns, grads, parts, hoops, sums = scratch
    xi_r, xi_z, eta_r, eta_z, weight, radius = rows
    rho = 1.0 / radius
    scale = weight * radius
    back = [scale * xi_r, scale * xi_z, scale * eta_r, scale * eta_z]
    lane = lax.broadcasted_iota(jnp.int32, (STRIP, 128), 1)
    plus = lane < NODES

    def product(high, low, a_hi, a_lo):
        both = dot(high, jnp.concatenate([a_hi, a_lo], axis=1))
        return both[:, 0:128] + both[:, 128:256] + dot(low, a_hi)

    for order in range(2):
        both = product(*block(order), *split(coefs[pl.ds(order, MODES, stride=2), :]))
        even_odd[:, 128 * order : 128 * order + 128] = both[0:HALF]
        turns[:, 128 * order : 128 * order + 128] = both[HALF : 2 * HALF]
    sign = 1.0 - 2.0 * (lax.broadcasted_iota(jnp.int32, (HALF, 128), 0) % 2).astype(f32)
    even_odd[:, 0:128] = even_odd[:, 0:128] + sign * coefs[1:2, :]

    high, low = split(even_odd[...])
    for i in range(3):
        b_hi, b_lo = block(6 + i)
        grads[:, 256 * i : 256 * i + 256] = dot(high, b_hi) + dot(low, b_hi) + dot(high, b_lo)

    def strip(k, _):
        here = pl.ds(pl.multiple_of(k * STRIP, STRIP), STRIP)
        even, odd = even_odd[here, 0:128], even_odd[here, 128:256]
        turned_odd, turned_even = turns[here, 0:128], turns[here, 128:256]
        u_plus, u_minus = even + odd, even - odd
        r_plus, r_minus = turned_even + turned_odd, turned_even - turned_odd
        v = [None] * 9
        for c in range(3):
            ax = grads[here, 128 * c : 128 * c + 128]
            ae = grads[here, 384 + 128 * c : 512 + 128 * c]
            v[c] = xi_r * ax + eta_r * ae
            v[3 + c] = xi_z * ax + eta_z * ae
        v[6] = jnp.where(plus, r_plus - turn(u_plus, -NODES), turn(r_minus, NODES) - u_minus)
        v[7] = jnp.where(plus, turn(r_plus, -NODES) + u_plus, r_minus + turn(u_minus, NODES))
        v[8] = jnp.where(plus, turn(r_plus, -2 * NODES), turn(r_minus, -NODES))
        deform = [
            [1.0 + v[0], rho * v[6], v[3]],
            [v[1], 1.0 + rho * v[7], v[4]],
            [v[2], rho * v[8], 1.0 + v[5]],
        ]
        cof = [
            [
                deform[(i + 1) % 3][(j + 1) % 3] * deform[(i + 2) % 3][(j + 2) % 3]
                - deform[(i + 1) % 3][(j + 2) % 3] * deform[(i + 2) % 3][(j + 1) % 3]
                for j in range(3)
            ]
            for i in range(3)
        ]
        volume = deform[0][0] * cof[0][0] + deform[0][1] * cof[0][1] + deform[0][2] * cof[0][2]
        factor = bulk * (volume - 1.0) - shear
        piola = [[shear * deform[i][j] + factor * cof[i][j] for j in range(3)] for i in range(3)]
        for c in range(3):
            for i, value in (
                (c, back[0] * piola[c][0] + back[1] * piola[c][2]),
                (3 + c, back[2] * piola[c][0] + back[3] * piola[c][2]),
            ):
                v_hi, v_lo = split(value)
                parts[here, 128 * i : 128 * i + 128] = v_hi
                parts[here, 768 + 128 * i : 896 + 128 * i] = v_lo
        hoop = [weight * piola[c][1] for c in range(3)]
        for i, sense in ((0, 1.0), (1, -1.0)):
            pair = [jnp.where(plus, h + sense * turn(h, -NODES), 0.0) for h in hoop]
            first = 256 * i
            hoops[here, first : first + 128] = pair[1] - turn(pair[0], NODES)
            hoops[here, first + 128 : first + 256] = (
                pair[0] + turn(pair[1], NODES) + turn(pair[2], 2 * NODES)
            )
        return 0

    lax.fori_loop(0, HALF // STRIP, strip, 0, unroll=True)

    high, low = parts[:, 0:768], parts[:, 768:1536]
    b_hi, b_lo = block(9)
    straight = dot(high, b_hi) + dot(low, b_hi) + dot(high, b_lo)
    even = straight[:, 0:128] + hoops[:, 0:128]
    odd = straight[:, 128:256] + hoops[:, 256:384]
    half = ANGLES // 2
    for i, value in enumerate((even, hoops[:, 384:512], odd, hoops[:, 128:256])):
        v_hi, v_lo = split(value[0:half])
        sums[half * i : half * i + half, 0:128] = v_hi
        sums[half * i : half * i + half, 128:256] = v_lo

    step = 2.0 * math.pi / ANGLES
    row = lax.broadcasted_iota(jnp.int32, (MODES, 128), 0)
    signed = (0.5 * step) * (1.0 - 2.0 * (row % 2).astype(f32))
    weights = jnp.where(row == 0, 0.5 * signed, signed) * 2.0
    last = jnp.sum(weights * even[0:half], axis=0, keepdims=True) + 0.5 * step * even[half : half + 1]
    pieces = [(sums[half * i : half * i + half, 0:128], sums[half * i : half * i + half, 128:256]) for i in range(4)]
    cos_part = product(*block(2), *pieces[0]) + product(*block(3), *pieces[1])
    result[pl.ds(0, MODES, stride=2), :] = cos_part + signed * even[half : half + 1]
    sin_part = product(*block(4), *pieces[2]) + product(*block(5), *pieces[3])
    sin_part = sin_part + (row.astype(f32) * signed) * hoops[half : half + 1, 128:256]
    result[pl.ds(1, MODES, stride=2), :] = jnp.where(row == 0, last, sin_part)


def kernel(
    disp_in, metric_in, weight_in, radius_in, moduli_in, neigh_in, side_in, pres_in,
    table_in,
    out,
    disp, metric, weights, radii, moduli, neigh, side, pres,
    pack, got1, got2, state1, result, back0, back1, home0, home1, perm, rims, rims_back, rim_out, rim_in, base, traces, partial,
    even_odd, turns, grads, parts, hoops, sums,
    table,
    relay1, relay2, relay3, relay4,
    disp_sem, small_sem, table_sem,
    s1, r1, m1, o1, s2, r2, m2, o2, s3, r3, m3, o3, s4, r4, m4, o4,
    rim_send, rim_recv,
):
    sems1, sems2, sems3, sems4 = (s1, r1, m1, o1), (s2, r2, m2, o2), (s3, r3, m3, o3), (s4, r4, m4, o4)
    elem = lax.axis_index("elem")
    mode = lax.axis_index("mode")
    runs = lax.axis_size("elem")
    half, rest = mode // 8, mode % 8
    row, core = rest // 2, rest % 2
    height = half * 8 + elem // 4

    def place(dz, dy, dc):
        there = (height + dz + 16) % 16
        column = (row + dy + 4) % 4 * 2 + (core + dc + 2) % 2
        return there % 8 * 4 + elem % 4, there // 8 * 8 + column

    disp_copies = [pltpu.make_async_copy(disp_in.at[s], disp.at[s], disp_sem.at[s]) for s in range(2)]
    for copy in disp_copies:
        copy.start()
    barrier = pltpu.get_barrier_semaphore()
    senders = [place(-LEG * up, -dy, -dc) for dy, dc, up in CROSS] + [place(LEG, 0, 0)]
    senders += [place(0, -dy, -dc) for dy, dc in LOCAL]
    for sender in senders:
        pl.semaphore_signal(barrier, inc=1, device_id=sender, device_id_type=MESH)

    @pl.when(elem > 0)
    def _():
        pl.semaphore_signal(barrier, inc=1, device_id=(elem - 1, mode), device_id_type=MESH)

    @pl.when(elem < runs - 1)
    def _():
        pl.semaphore_signal(barrier, inc=1, device_id=(elem + 1, mode), device_id_type=MESH)

    small_copies = [
        pltpu.make_async_copy(src, dst, small_sem.at[i])
        for i, (src, dst) in enumerate(
            [(metric_in, metric), (weight_in, weights), (radius_in, radii), (moduli_in, moduli),
             (neigh_in, neigh), (side_in, side), (pres_in, pres)]
        )
    ]
    for copy in small_copies:
        copy.start()

    lane = lax.broadcasted_iota(jnp.int32, (OWN, 128), 1)
    lane8 = lax.broadcasted_iota(jnp.int32, (8, 128), 1)

    def column(s, c, g):
        if g < 4:
            return disp[s, c, :, 128 * g : 128 * g + 128]
        return jnp.concatenate([disp[s, c, :, 512:576], jnp.zeros((OWN, 64), f32)], axis=1)

    def gather_element(s, j, base_lane):
        result = jnp.zeros((OWN, 128), f32)
        for c in range(3):
            target = NODES * c + base_lane
            first = NODES * j
            for g in range(first // 128, (first + NODES - 1) // 128 + 1):
                low = max(first, 128 * g)
                high = min(first + NODES, 128 * g + 128)
                moved = turn(column(s, c, g), target - (first - 128 * g))
                begin = (target + low - first) % 128
                end = begin + high - low
                inside = (lane >= begin) & (lane < end)
                if end > 128:
                    inside = (lane >= begin) | (lane < end - 128)
                result = jnp.where(inside, moved, result)
        return result

    def pack_rows(full, ragged):
        last = ragged[24:32]
        tails = [turn(last, 88), turn(last, 48), turn(last, 8)]
        rows = [jnp.where(lane8 < 88, ragged[8 * t : 8 * t + 8], tails[t]) for t in range(3)]
        return jnp.where(lane < 108, full, ragged), jnp.concatenate(rows, axis=0)

    def unpack_ragged(first, second):
        rows = [
            jnp.where(lane8 < 88, second[8 * t : 8 * t + 8], first[8 * t : 8 * t + 8]) for t in range(3)
        ]
        moved = [turn(second[0:8], -88), turn(second[8:16], -48), turn(second[16:24], -8)]
        last = jnp.where(lane8 < 40, moved[0], jnp.where(lane8 < 80, moved[1], moved[2]))
        rows.append(jnp.where(lane8 < 88, last, first[24:32]))
        return jnp.concatenate(rows, axis=0)

    for copy in disp_copies:
        copy.wait()
    for j in range(PEERS):
        full = gather_element(0, j, 0)
        ragged = gather_element(1, j, 108)
        top, bottom = pack_rows(full, ragged)
        pack[j, 0:32, :] = top
        pack[j, 32:56, :] = bottom

    table_copy = pltpu.make_async_copy(table_in, table, table_sem)
    table_copy.start()

    neighbours_there = 2 - (elem == 0).astype(jnp.int32) - (elem == runs - 1).astype(jnp.int32)
    pl.semaphore_wait(barrier, len(senders) + neighbours_there)

    class Exchange:
        def __init__(self, source, target, arrivals, relay, sems):
            send, recv, relayed, onward = sems
            self.all = arrivals, relay, send, recv, onward
            self.first, self.second, self.local = [], [], []
            for i, (dy, dc, up) in enumerate(CROSS):
                owner = place(2 * LEG, dy, dc)[1]
                origin = place(-LEG * up, 0, 0)[1]
                self.first.append(
                    pltpu.make_async_remote_copy(
                        src_ref=source(owner), dst_ref=relay.at[i],
                        send_sem=send, recv_sem=relayed.at[i],
                        device_id=place(LEG * up, 0, 0), device_id_type=MESH,
                    )
                )
                self.second.append(
                    pltpu.make_async_remote_copy(
                        src_ref=relay.at[i], dst_ref=target(origin),
                        send_sem=onward, recv_sem=recv,
                        device_id=place(LEG * up, dy, dc), device_id_type=MESH,
                    )
                )
            for i, (dy, dc) in enumerate(LOCAL):
                to = place(0, dy, dc)
                self.local.append(
                    pltpu.make_async_remote_copy(
                        src_ref=source(to[1]), dst_ref=target(mode),
                        send_sem=send, recv_sem=recv,
                        device_id=to, device_id_type=MESH,
                    )
                )

        def start(self):
            for copy in self.first + self.local:
                copy.start()

        def forward(self):
            for first, second in zip(self.first, self.second):
                first.wait_recv()
                second.start()

        def arrive(self):
            arrivals, _, _, recv, _ = self.all
            pltpu.make_async_copy(arrivals, arrivals, recv).wait()

        def finish(self):
            arrivals, relay, send, _, onward = self.all
            pltpu.make_async_copy(arrivals, arrivals, send).wait()
            pltpu.make_async_copy(relay, relay, onward).wait()

    def full_rows(me):
        return got1.at[pl.ds(pl.multiple_of(me * OWN, OWN), OWN)]

    there1 = Exchange(lambda to: pack.at[to, 0:32], full_rows, got1.at[0 : 15 * OWN], relay1, sems1)
    there2 = Exchange(lambda to: pack.at[to, 32:56], lambda me: got2.at[me], got2.at[0:15], relay2, sems2)
    again0 = Exchange(lambda to: back0.at[to], lambda me: home0.at[me], home0.at[0:15], relay3, sems3)
    again1 = Exchange(lambda to: back1.at[to], lambda me: home1.at[me], home1.at[0:15], relay4, sems4)
    there1.start()
    there2.start()
    got1[pl.ds(pl.multiple_of(mode * OWN, OWN), OWN), :] = pack[mode, 0:32, :]
    got2[mode] = pack[mode, 32:56, :]

    for copy in small_copies:
        copy.wait()

    def wide(pieces):
        return jnp.concatenate(pieces + [jnp.zeros((1, WIDE - POINTS), f32)], axis=1)

    def as_row(ref):
        return wide([ref[128 * g : min(128 * g + 128, POINTS)].reshape(1, -1) for g in range(5)])

    geo = [wide([metric[i : i + 1, :]]) for i in range(4)] + [as_row(weights), as_row(radii)]
    stacked = jnp.concatenate(geo + [jnp.zeros((2, WIDE), f32)], axis=0)
    stacked = pltpu.roll(stacked, (WIDE - NODES * mode) % WIDE, 1)

    def own_row(i):
        return stacked[i : i + 1, 0:128]

    lane1 = lax.broadcasted_iota(jnp.int32, (1, 128), 1)
    own = [jnp.where(lane1 < NODES, own_row(i), 0.0) for i in range(6)]
    own = [r + turn(r, NODES) for r in own]
    own[5] = jnp.where(lane1 < 2 * NODES, own[5], 1.0)
    shear = moduli[0, mode]
    bulk = moduli[1, mode]

    first_elem = elem * PEERS
    head = jnp.int32(0)
    tail = jnp.int32(0)
    point = lax.broadcasted_iota(jnp.int32, (1, WIDE), 1)
    e_lane = sum((point >= NODES * i).astype(jnp.int32) for i in range(1, PEERS + 1))
    inner = point - NODES * e_lane
    a_lane = sum((inner >= 6 * i).astype(jnp.int32) for i in range(1, 6))
    b_lane = inner - 6 * a_lane
    partner = jnp.full((1, WIDE), -1, jnp.int32)
    sides = jnp.zeros((1, WIDE), jnp.int32)
    for e in range(PEERS):
        prev = neigh[0, e] - first_elem
        nxt = neigh[1, e] - first_elem
        prev_here = (prev >= 0) & (prev < PEERS)
        next_here = (nxt >= 0) & (nxt < PEERS)
        head = head + jnp.where(prev_here, 0, e)
        tail = tail + jnp.where(next_here, 0, e)
        low = jnp.where(prev_here, prev * NODES + 5, -10000)
        high = jnp.where(next_here, nxt * NODES, -10000)
        here = e_lane == e
        partner = jnp.where(here & (b_lane == 0), low + 6 * a_lane, partner)
        partner = jnp.where(here & (b_lane == 5), high + 6 * a_lane, partner)
        sides = jnp.where(here, side[e], sides)
    for g in range(5):
        rows = lax.broadcasted_iota(jnp.int32, (128, WIDE), 0) + 128 * g
        perm[128 * g : 128 * g + 128, :] = jnp.where(rows == partner, 1.0, 0.0).astype(bf16)
    slot = sum((lane1 >= 6 * i).astype(jnp.int32) for i in range(1, 13))
    node = lane1 - 6 * slot
    head_node = jnp.where(slot < 12, head * NODES + 6 * node, -1)
    tail_node = jnp.where(slot < 12, tail * NODES + 6 * node + 5, -1)
    for g in range(5):
        rows = lax.broadcasted_iota(jnp.int32, (128, 128), 0) + 128 * g
        rims[128 * g : 128 * g + 128, 0:128] = jnp.where(rows == head_node, 1.0, 0.0).astype(bf16)
        rims[128 * g : 128 * g + 128, 128:256] = jnp.where(rows == tail_node, 1.0, 0.0).astype(bf16)
    line = lax.broadcasted_iota(jnp.int32, (128, WIDE), 0)
    line_slot = sum((line >= 6 * i).astype(jnp.int32) for i in range(1, 13))
    line_node = 6 * (line - 6 * line_slot)
    line_used = line_slot < 12
    for way, first in ((0, head * NODES), (1, tail * NODES + 5)):
        match = line_used & (point == first + line_node)
        rims_back[128 * way : 128 * way + 128, :] = jnp.where(match, 1.0, 0.0).astype(bf16)
    facing = (a_lane == 5 * sides) & (e_lane < PEERS)
    outward = (2 * sides - 1).astype(f32)
    face = jnp.where(facing, 15.0 * outward * geo[4] * geo[5], 0.0)
    order = lax.broadcasted_iota(jnp.int32, (OWN, 128), 0)
    pressure = jnp.zeros((OWN, 128), f32)
    for i in range(OWN):
        pressure = jnp.where(order == i, pres[i], pressure)
    for g in range(5):
        columns = slice(128 * g, 128 * g + 128)
        base[0, :, columns] = pressure * (face * geo[0])[:, columns]
        base[1, :, columns] = pressure * (face * geo[1])[:, columns]

    table_copy.wait()

    scratch = (even_odd, turns, grads, parts, hoops, sums)

    there1.forward()
    there2.forward()
    there1.arrive()

    evaluate(got1, result, own, shear, bulk, table, scratch)
    for i in range(PEERS):
        block = turn(result[OWN * i : OWN * i + OWN, :], 108)
        _, bottom = pack_rows(block, block)
        back0[i] = bottom
        back1[i] = block
    again0.start()
    home0[mode] = back0[mode]

    there2.arrive()
    for i in range(PEERS):
        state1[OWN * i : OWN * i + OWN, :] = turn(unpack_ragged(got1[OWN * i : OWN * i + OWN, :], got2[i]), 20)

    evaluate(state1, result, own, shear, bulk, table, scratch)
    for i in range(PEERS):
        back1[i] = jnp.where(lane < 108, result[OWN * i : OWN * i + OWN, :], back1[i])
    again1.start()
    home1[mode] = back1[mode]

    again0.forward()
    again1.forward()
    def side_by_side(pieces, c):
        columns = []
        for g in range(5):
            acc = jnp.zeros((OWN, 128), f32)
            for i in range(PEERS):
                low = max(NODES * i, 128 * g) - 128 * g
                high = min(NODES * i + NODES, 128 * g + 128) - 128 * g
                if low < high:
                    moved = turn(pieces[i], NODES * i - 128 * g - NODES * c)
                    acc = jnp.where((lane >= low) & (lane < high), moved, acc)
            columns.append(acc)
        whole = jnp.concatenate(columns, axis=1)
        return whole if c == 1 else whole + base[c // 2]

    def assemble(first, l_hi, l_lo, loaded):
        rows = slice(first, first + loaded.shape[0])
        partial[rows, :] = loaded + dot(l_hi, perm[...]) + dot(l_lo, perm[...])

    def trace(first, l_hi, l_lo):
        rows = slice(first, first + l_hi.shape[0])
        traces[rows, :] = dot(l_hi, rims[...]) + dot(l_lo, rims[...])

    again0.arrive()
    early = [turn(unpack_ragged(back1[i], home0[i]), 20) for i in range(PEERS)]
    early = jnp.concatenate([side_by_side(early, 1), side_by_side(early, 2)], axis=0)
    early_parts = split(early)
    trace(0, *early_parts)
    assemble(0, *early_parts, early)
    again1.arrive()
    late = [turn(unpack_ragged(home1[i], home0[i]), 20) for i in range(PEERS)]
    late = [side_by_side(late, 0)] + [side_by_side([home1[i] for i in range(PEERS)], c) for c in range(3)]
    late = jnp.concatenate(late, axis=0)
    late_parts = split(late)
    trace(64, *late_parts)

    for way in range(2):
        columns = slice(128 * way, 128 * way + 128)
        for s in range(2):
            tile = jnp.zeros((8, 128), f32)
            for t in range(12):
                tile = jnp.where(slot == t, traces[96 * s + 8 * t : 96 * s + 8 * t + 8, columns], tile)
            rim_out[way, 8 * s : 8 * s + 8, :] = tile

    to_prev = pltpu.make_async_remote_copy(
        src_ref=rim_out.at[0], dst_ref=rim_in.at[1], send_sem=rim_send.at[0], recv_sem=rim_recv.at[1],
        device_id=(jnp.maximum(elem - 1, 0), mode), device_id_type=MESH,
    )
    to_next = pltpu.make_async_remote_copy(
        src_ref=rim_out.at[1], dst_ref=rim_in.at[0], send_sem=rim_send.at[1], recv_sem=rim_recv.at[0],
        device_id=(jnp.minimum(elem + 1, runs - 1), mode), device_id_type=MESH,
    )

    @pl.when(elem > 0)
    def _():
        to_prev.start()

    @pl.when(elem < runs - 1)
    def _():
        to_next.start()

    assemble(64, *late_parts, late)

    @pl.when(elem > 0)
    def _():
        to_next.wait_recv()

    @pl.when(elem < runs - 1)
    def _():
        to_prev.wait_recv()

    arrived = []
    for way, there in ((0, elem > 0), (1, elem < runs - 1)):
        rows = []
        for s in range(2):
            tile = jnp.where(there, rim_in[way, 8 * s : 8 * s + 8, :], 0.0)
            rows += [jnp.where(slot == t, tile, 0.0) for t in range(12)]
        arrived.append(jnp.concatenate(rows, axis=0))
    a_hi, a_lo = split(jnp.concatenate(arrived, axis=1))
    places = [(0, 1), (0, 2), (0, 0), (1, 0), (1, 1), (1, 2)]
    for s in range(2):
        half_rows = slice(96 * s, 96 * s + 96)
        block = partial[half_rows, :] + dot(a_hi[half_rows], rims_back[...]) + dot(a_lo[half_rows], rims_back[...])
        for i in range(3):
            out[places[3 * s + i]] = block[32 * i : 32 * i + 32, 0:POINTS]
    for exchange in (there1, there2, again0, again1):
        exchange.finish()

    @pl.when(elem > 0)
    def _():
        to_prev.wait_send()

    @pl.when(elem < runs - 1)
    def _():
        to_next.wait_send()


EVALUATE_SCRATCH = [
    pltpu.VMEM((HALF, 256), f32),
    pltpu.VMEM((HALF, 256), f32),
    pltpu.VMEM((HALF, 768), f32),
    pltpu.VMEM((HALF, 1536), bf16),
    pltpu.VMEM((HALF, 512), f32),
    pltpu.VMEM((2 * ANGLES, 256), bf16),
]


def on_device(displacement, metric, weight_jac, radius, moduli, neighbours, inner_side, pressure):
    table = jnp.asarray(tables())
    hbm, vmem = pl.BlockSpec(memory_space=pltpu.HBM), pl.BlockSpec(memory_space=pltpu.VMEM)
    single = pltpu.SemaphoreType.DMA
    sems = [single, single, pltpu.SemaphoreType.DMA((len(CROSS),)), single]
    return pl.pallas_call(
        kernel,
        out_shape=jax.ShapeDtypeStruct((2, 3, OWN, POINTS), f32),
        in_specs=[hbm] * 9,
        out_specs=vmem,
        scratch_shapes=[
            pltpu.VMEM((2, 3, OWN, POINTS), f32),
            pltpu.VMEM((4, POINTS), f32),
            pltpu.VMEM((POINTS,), f32),
            pltpu.VMEM((POINTS,), f32),
            pltpu.SMEM((2, PEERS), f32),
            pltpu.SMEM((2, PEERS), jnp.int32),
            pltpu.SMEM((PEERS,), jnp.int32),
            pltpu.SMEM((OWN,), f32),
            pltpu.VMEM((PEERS, 56, 128), f32),
            pltpu.VMEM((COEFS, 128), f32),
            pltpu.VMEM((PEERS, 24, 128), f32),
            pltpu.VMEM((COEFS, 128), f32),
            pltpu.VMEM((COEFS, 128), f32),
            pltpu.VMEM((PEERS, 24, 128), f32),
            pltpu.VMEM((PEERS, 32, 128), f32),
            pltpu.VMEM((PEERS, 24, 128), f32),
            pltpu.VMEM((PEERS, 32, 128), f32),
            pltpu.VMEM((WIDE, WIDE), bf16),
            pltpu.VMEM((WIDE, 256), bf16),
            pltpu.VMEM((256, WIDE), bf16),
            pltpu.VMEM((2, 16, 128), f32),
            pltpu.VMEM((2, 16, 128), f32),
            pltpu.VMEM((2, OWN, WIDE), f32),
            pltpu.VMEM((192, 256), f32),
            pltpu.VMEM((192, WIDE), f32),
            *EVALUATE_SCRATCH,
            pltpu.VMEM(table.shape, bf16),
            *[pltpu.VMEM((len(CROSS), n, 128), f32) for n in (32, 24, 24, 32)],
            pltpu.SemaphoreType.DMA((2,)),
            pltpu.SemaphoreType.DMA((7,)),
            pltpu.SemaphoreType.DMA,
            *sems * 4,
            pltpu.SemaphoreType.DMA((2,)),
            pltpu.SemaphoreType.DMA((2,)),
        ],
        compiler_params=pltpu.CompilerParams(
            collective_id=0, has_side_effects=True, vmem_limit_bytes=64 * 2**20
        ),
        name="bellows",
    )(
        displacement, metric, weight_jac, radius, moduli, neighbours.T, inner_side, pressure,
        table,
    )


def solution(mesh):
    placed = (
        P(None, None, "mode", "elem"),
        P(None, "elem"),
        P("elem"),
        P("elem"),
        P(None, "elem"),
        P("elem", None),
        P("elem"),
        P("mode"),
    )
    return jax.shard_map(
        on_device,
        mesh=mesh,
        in_specs=placed,
        out_specs=P(None, None, "mode", "elem"),
        check_vma=False,
    )
```

```python
import math

import jax
import jax.numpy as jnp
import ml_dtypes
import numpy as np
from jax import lax
from jax.experimental import pallas as pl
from jax.experimental.pallas import tpu as pltpu
from jax.sharding import PartitionSpec as P

MODES = 256
ANGLES = 512
COEFS = 512
NODES = 36
PEERS = 16
OWN = 32
POINTS = 576
WIDE = 640
HALF = 272
STRIP = 16
MESH = pl.DeviceIdType.MESH
f32, bf16 = jnp.float32, jnp.bfloat16

LOCAL = [(dy, dc) for dy in (2, 1, 3, 0) for dc in (1, 0) if dy + dc]
CROSS = [(dy, dc, 1 - (dy + dc) % 2 * 2) for dy in (2, 1, 3, 0) for dc in (0, 1)]
LEG = 4


def line_derivative():
    inner_node = math.sqrt(1.0 / 3.0 - 2.0 * math.sqrt(7.0) / 21.0)
    outer_node = math.sqrt(1.0 / 3.0 + 2.0 * math.sqrt(7.0) / 21.0)
    gll_nodes = np.array([-1.0, -outer_node, -inner_node, inner_node, outer_node, 1.0])
    weights = np.array(
        [1.0 / np.prod([gll_nodes[j] - gll_nodes[k] for k in range(6) if k != j]) for j in range(6)]
    )
    derivative = np.zeros((6, 6))
    for i in range(6):
        for j in range(6):
            if i != j:
                derivative[i, j] = weights[j] / weights[i] / (gll_nodes[i] - gll_nodes[j])
        derivative[i, i] = -np.sum(derivative[i])
    return derivative


def halves(table):
    high = table.astype(np.float32).astype(ml_dtypes.bfloat16)
    low = (table - high.astype(np.float64)).astype(np.float32).astype(ml_dtypes.bfloat16)
    return high, low


def tables():
    counts = np.arange(HALF)
    orders = np.arange(MODES)
    phases = (counts[:, None] * orders[None, :] % ANGLES) * (2.0 * math.pi / ANGLES)
    used = (counts <= ANGLES // 2)[:, None]
    cosines, sines = np.cos(phases) * used, np.sin(phases) * used
    from_cos = np.concatenate([cosines, -orders * sines], axis=0)
    from_sin = np.concatenate([sines, orders * cosines], axis=0)
    step = 2.0 * math.pi / ANGLES
    ends = np.where(counts == 0, 0.5, 1.0)[: ANGLES // 2, None]
    cosines, sines = step * ends * cosines[: ANGLES // 2], step * sines[: ANGLES // 2]
    to_cos = np.concatenate([cosines, -orders * sines], axis=0).T
    to_sin = np.concatenate([sines, orders * cosines], axis=0).T
    derivative = line_derivative()
    slopes = [np.kron(derivative, np.eye(6)).T, np.kron(np.eye(6), derivative).T]
    spread = np.zeros((256, 768))
    for way, slope in enumerate(slopes):
        for c in range(3):
            column = 384 * way + 128 * c
            even, odd = NODES * c, 128 + NODES * c
            spread[even : even + NODES, column : column + 2 * NODES] = np.concatenate([slope, slope], axis=1)
            spread[odd : odd + NODES, column : column + 2 * NODES] = np.concatenate([slope, -slope], axis=1)
    blocks = [from_cos, from_sin, to_cos[:, 0:256], to_cos[:, 256:512], to_sin[:, 0:256], to_sin[:, 256:512]]
    blocks += [spread[:, 0:256], spread[:, 256:512], spread[:, 512:768], spread.T]
    return np.concatenate([part for block in blocks for part in halves(block)], axis=0)


BLOCK_ROWS = [2 * HALF] * 2 + [256] * 4 + [256] * 3 + [768]
BLOCK_START = np.concatenate([[0], np.cumsum([2 * n for n in BLOCK_ROWS])]).tolist()


def split(values):
    high = values.astype(bf16)
    return high, (values - high.astype(f32)).astype(bf16)


def dot(a, b):
    return jnp.dot(a, b, preferred_element_type=f32)


def turn(values, shift):
    shift = shift % 128
    return pltpu.roll(values, shift, 1) if shift else values


def evaluate(coefs, result, rows, shear, bulk, table, scratch):
    def block(i):
        first, count = BLOCK_START[i], BLOCK_ROWS[i]
        return table[first : first + count, :], table[first + count : first + 2 * count, :]

    even_odd, turns, grads, parts, hoops, sums = scratch
    xi_r, xi_z, eta_r, eta_z, weight, radius = rows
    rho = 1.0 / radius
    scale = weight * radius
    back = [scale * xi_r, scale * xi_z, scale * eta_r, scale * eta_z]
    lane = lax.broadcasted_iota(jnp.int32, (STRIP, 128), 1)
    plus = lane < NODES

    def product(high, low, a_hi, a_lo):
        both = dot(high, jnp.concatenate([a_hi, a_lo], axis=1))
        return both[:, 0:128] + both[:, 128:256] + dot(low, a_hi)

    for order in range(2):
        both = product(*block(order), *split(coefs[pl.ds(order, MODES, stride=2), :]))
        even_odd[:, 128 * order : 128 * order + 128] = both[0:HALF]
        turns[:, 128 * order : 128 * order + 128] = both[HALF : 2 * HALF]
    sign = 1.0 - 2.0 * (lax.broadcasted_iota(jnp.int32, (HALF, 128), 0) % 2).astype(f32)
    even_odd[:, 0:128] = even_odd[:, 0:128] + sign * coefs[1:2, :]

    high, low = split(even_odd[...])
    for i in range(3):
        b_hi, b_lo = block(6 + i)
        grads[:, 256 * i : 256 * i + 256] = dot(high, b_hi) + dot(low, b_hi) + dot(high, b_lo)

    def strip(k, _):
        here = pl.ds(pl.multiple_of(k * STRIP, STRIP), STRIP)
        even, odd = even_odd[here, 0:128], even_odd[here, 128:256]
        turned_odd, turned_even = turns[here, 0:128], turns[here, 128:256]
        u_plus, u_minus = even + odd, even - odd
        r_plus, r_minus = turned_even + turned_odd, turned_even - turned_odd
        v = [None] * 9
        for c in range(3):
            ax = grads[here, 128 * c : 128 * c + 128]
            ae = grads[here, 384 + 128 * c : 512 + 128 * c]
            v[c] = xi_r * ax + eta_r * ae
            v[3 + c] = xi_z * ax + eta_z * ae
        v[6] = jnp.where(plus, r_plus - turn(u_plus, -NODES), turn(r_minus, NODES) - u_minus)
        v[7] = jnp.where(plus, turn(r_plus, -NODES) + u_plus, r_minus + turn(u_minus, NODES))
        v[8] = jnp.where(plus, turn(r_plus, -2 * NODES), turn(r_minus, -NODES))
        deform = [
            [1.0 + v[0], rho * v[6], v[3]],
            [v[1], 1.0 + rho * v[7], v[4]],
            [v[2], rho * v[8], 1.0 + v[5]],
        ]
        cof = [
            [
                deform[(i + 1) % 3][(j + 1) % 3] * deform[(i + 2) % 3][(j + 2) % 3]
                - deform[(i + 1) % 3][(j + 2) % 3] * deform[(i + 2) % 3][(j + 1) % 3]
                for j in range(3)
            ]
            for i in range(3)
        ]
        volume = deform[0][0] * cof[0][0] + deform[0][1] * cof[0][1] + deform[0][2] * cof[0][2]
        factor = bulk * (volume - 1.0) - shear
        piola = [[shear * deform[i][j] + factor * cof[i][j] for j in range(3)] for i in range(3)]
        for c in range(3):
            for i, value in (
                (c, back[0] * piola[c][0] + back[1] * piola[c][2]),
                (3 + c, back[2] * piola[c][0] + back[3] * piola[c][2]),
            ):
                v_hi, v_lo = split(value)
                parts[here, 128 * i : 128 * i + 128] = v_hi
                parts[here, 768 + 128 * i : 896 + 128 * i] = v_lo
        hoop = [weight * piola[c][1] for c in range(3)]
        for i, sense in ((0, 1.0), (1, -1.0)):
            pair = [jnp.where(plus, h + sense * turn(h, -NODES), 0.0) for h in hoop]
            first = 256 * i
            hoops[here, first : first + 128] = pair[1] - turn(pair[0], NODES)
            hoops[here, first + 128 : first + 256] = (
                pair[0] + turn(pair[1], NODES) + turn(pair[2], 2 * NODES)
            )
        return 0

    lax.fori_loop(0, HALF // STRIP, strip, 0, unroll=True)

    high, low = parts[:, 0:768], parts[:, 768:1536]
    b_hi, b_lo = block(9)
    straight = dot(high, b_hi) + dot(low, b_hi) + dot(high, b_lo)
    even = straight[:, 0:128] + hoops[:, 0:128]
    odd = straight[:, 128:256] + hoops[:, 256:384]
    half = ANGLES // 2
    for i, value in enumerate((even, hoops[:, 384:512], odd, hoops[:, 128:256])):
        v_hi, v_lo = split(value[0:half])
        sums[half * i : half * i + half, 0:128] = v_hi
        sums[half * i : half * i + half, 128:256] = v_lo

    step = 2.0 * math.pi / ANGLES
    row = lax.broadcasted_iota(jnp.int32, (MODES, 128), 0)
    signed = (0.5 * step) * (1.0 - 2.0 * (row % 2).astype(f32))
    weights = jnp.where(row == 0, 0.5 * signed, signed) * 2.0
    last = jnp.sum(weights * even[0:half], axis=0, keepdims=True) + 0.5 * step * even[half : half + 1]
    pieces = [(sums[half * i : half * i + half, 0:128], sums[half * i : half * i + half, 128:256]) for i in range(4)]
    cos_part = product(*block(2), *pieces[0]) + product(*block(3), *pieces[1])
    result[pl.ds(0, MODES, stride=2), :] = cos_part + signed * even[half : half + 1]
    sin_part = product(*block(4), *pieces[2]) + product(*block(5), *pieces[3])
    sin_part = sin_part + (row.astype(f32) * signed) * hoops[half : half + 1, 128:256]
    result[pl.ds(1, MODES, stride=2), :] = jnp.where(row == 0, last, sin_part)


def kernel(
    disp_in, metric_in, weight_in, radius_in, moduli_in, neigh_in, side_in, pres_in,
    table_in,
    out,
    disp, metric, weights, radii, moduli, neigh, side, pres,
    pack, got1, got2, state1, result, back0, back1, home0, home1, perm, rims, rims_back, rim_out, rim_in, base, traces, partial,
    even_odd, turns, grads, parts, hoops, sums,
    table,
    relay1,
    disp_sem, small_sem, table_sem,
    s1, r1, m1, o1, s2, r2, s3, r3, s4, r4, far,
    rim_send, rim_recv,
):
    sems1, sems2, sems3, sems4 = (s1, r1, m1, o1), (s2, r2, None, None), (s3, r3, None, None), (s4, r4, None, None)
    elem = lax.axis_index("elem")
    mode = lax.axis_index("mode")
    runs = lax.axis_size("elem")
    half, rest = mode // 8, mode % 8
    row, core = rest // 2, rest % 2
    height = half * 8 + elem // 4

    def place(dz, dy, dc):
        there = (height + dz + 16) % 16
        column = (row + dy + 4) % 4 * 2 + (core + dc + 2) % 2
        return there % 8 * 4 + elem % 4, there // 8 * 8 + column

    disp_copies = [pltpu.make_async_copy(disp_in.at[s], disp.at[s], disp_sem.at[s]) for s in range(2)]
    for copy in disp_copies:
        copy.start()
    barrier = pltpu.get_barrier_semaphore()
    senders = [place(-LEG * up, -dy, -dc) for dy, dc, up in CROSS] + [place(LEG, 0, 0)]
    senders += [place(0, -dy, -dc) for dy, dc in LOCAL]
    for sender in senders:
        pl.semaphore_signal(barrier, inc=1, device_id=sender, device_id_type=MESH)

    @pl.when(elem > 0)
    def _():
        pl.semaphore_signal(barrier, inc=1, device_id=(elem - 1, mode), device_id_type=MESH)

    @pl.when(elem < runs - 1)
    def _():
        pl.semaphore_signal(barrier, inc=1, device_id=(elem + 1, mode), device_id_type=MESH)

    small_copies = [
        pltpu.make_async_copy(src, dst, small_sem.at[i])
        for i, (src, dst) in enumerate(
            [(metric_in, metric), (weight_in, weights), (radius_in, radii), (moduli_in, moduli),
             (neigh_in, neigh), (side_in, side), (pres_in, pres)]
        )
    ]
    for copy in small_copies:
        copy.start()

    lane = lax.broadcasted_iota(jnp.int32, (OWN, 128), 1)
    lane8 = lax.broadcasted_iota(jnp.int32, (8, 128), 1)

    def column(s, c, g):
        if g < 4:
            return disp[s, c, :, 128 * g : 128 * g + 128]
        return jnp.concatenate([disp[s, c, :, 512:576], jnp.zeros((OWN, 64), f32)], axis=1)

    def gather_element(s, j, base_lane):
        result = jnp.zeros((OWN, 128), f32)
        for c in range(3):
            target = NODES * c + base_lane
            first = NODES * j
            for g in range(first // 128, (first + NODES - 1) // 128 + 1):
                low = max(first, 128 * g)
                high = min(first + NODES, 128 * g + 128)
                moved = turn(column(s, c, g), target - (first - 128 * g))
                begin = (target + low - first) % 128
                end = begin + high - low
                inside = (lane >= begin) & (lane < end)
                if end > 128:
                    inside = (lane >= begin) | (lane < end - 128)
                result = jnp.where(inside, moved, result)
        return result

    def pack_rows(full, ragged):
        last = ragged[24:32]
        tails = [turn(last, 88), turn(last, 48), turn(last, 8)]
        rows = [jnp.where(lane8 < 88, ragged[8 * t : 8 * t + 8], tails[t]) for t in range(3)]
        return jnp.where(lane < 108, full, ragged), jnp.concatenate(rows, axis=0)

    def unpack_ragged(first, second):
        rows = [
            jnp.where(lane8 < 88, second[8 * t : 8 * t + 8], first[8 * t : 8 * t + 8]) for t in range(3)
        ]
        moved = [turn(second[0:8], -88), turn(second[8:16], -48), turn(second[16:24], -8)]
        last = jnp.where(lane8 < 40, moved[0], jnp.where(lane8 < 80, moved[1], moved[2]))
        rows.append(jnp.where(lane8 < 88, last, first[24:32]))
        return jnp.concatenate(rows, axis=0)

    for copy in disp_copies:
        copy.wait()
    for j in range(PEERS):
        full = gather_element(0, j, 0)
        ragged = gather_element(1, j, 108)
        top, bottom = pack_rows(full, ragged)
        pack[j, 0:32, :] = top
        pack[j, 32:56, :] = bottom

    table_copy = pltpu.make_async_copy(table_in, table, table_sem)
    table_copy.start()

    neighbours_there = 2 - (elem == 0).astype(jnp.int32) - (elem == runs - 1).astype(jnp.int32)
    pl.semaphore_wait(barrier, len(senders) + neighbours_there)

    class Exchange:
        def __init__(self, source, target, arrivals, sems, relay=None):
            send, recv, relayed, onward = sems
            self.all = arrivals, relay, send, recv, onward
            self.first, self.second = [], []

            def copy(src, dst, sent, received, to):
                return pltpu.make_async_remote_copy(
                    src_ref=src, dst_ref=dst, send_sem=sent, recv_sem=received,
                    device_id=to, device_id_type=MESH,
                )

            for i, (dy, dc, up) in enumerate(CROSS):
                owner = place(2 * LEG, dy, dc)
                if relay is None:
                    self.first.append(copy(source(owner[1]), target(mode), send, recv, owner))
                    continue
                origin = place(-LEG * up, 0, 0)[1]
                self.first.append(copy(source(owner[1]), relay.at[i], send, relayed.at[i], place(LEG * up, 0, 0)))
                self.second.append(copy(relay.at[i], target(origin), onward, recv, place(LEG * up, dy, dc)))
            for dy, dc in LOCAL:
                to = place(0, dy, dc)
                self.first.append(copy(source(to[1]), target(mode), send, recv, to))

        def start(self):
            for one in self.first:
                one.start()

        def forward(self, low=0, high=8):
            for first, second in zip(self.first[low:high], self.second[low:high]):
                first.wait_recv()
                second.start()

        def arrive(self):
            arrivals, _, _, recv, _ = self.all
            pltpu.make_async_copy(arrivals, arrivals, recv).wait()

        def finish(self):
            arrivals, relay, send, _, onward = self.all
            pltpu.make_async_copy(arrivals, arrivals, send).wait()
            if relay is not None:
                pltpu.make_async_copy(relay, relay, onward).wait()

    def full_rows(me):
        return got1.at[pl.ds(pl.multiple_of(me * OWN, OWN), OWN)]

    there1 = Exchange(lambda to: pack.at[to, 0:32], full_rows, got1.at[0 : 15 * OWN], sems1, relay1)
    there2 = Exchange(lambda to: pack.at[to, 32:56], lambda me: got2.at[me], got2.at[0:15], sems2)
    again0 = Exchange(lambda to: back0.at[to], lambda me: home0.at[me], home0.at[0:15], sems3)
    again1 = Exchange(lambda to: back1.at[to], lambda me: home1.at[me], home1.at[0:15], sems4)
    there1.start()
    for dz in (LEG, -LEG):
        pl.semaphore_signal(far, inc=1, device_id=place(dz, 0, 0), device_id_type=MESH)
    got1[pl.ds(pl.multiple_of(mode * OWN, OWN), OWN), :] = pack[mode, 0:32, :]
    got2[mode] = pack[mode, 32:56, :]

    for copy in small_copies:
        copy.wait()

    def wide(pieces):
        return jnp.concatenate(pieces + [jnp.zeros((1, WIDE - POINTS), f32)], axis=1)

    def as_row(ref):
        return wide([ref[128 * g : min(128 * g + 128, POINTS)].reshape(1, -1) for g in range(5)])

    geo = [wide([metric[i : i + 1, :]]) for i in range(4)] + [as_row(weights), as_row(radii)]
    stacked = jnp.concatenate(geo + [jnp.zeros((2, WIDE), f32)], axis=0)
    stacked = pltpu.roll(stacked, (WIDE - NODES * mode) % WIDE, 1)

    def own_row(i):
        return stacked[i : i + 1, 0:128]

    lane1 = lax.broadcasted_iota(jnp.int32, (1, 128), 1)
    own = [jnp.where(lane1 < NODES, own_row(i), 0.0) for i in range(6)]
    own = [r + turn(r, NODES) for r in own]
    own[5] = jnp.where(lane1 < 2 * NODES, own[5], 1.0)
    shear = moduli[0, mode]
    bulk = moduli[1, mode]

    first_elem = elem * PEERS
    head = jnp.int32(0)
    tail = jnp.int32(0)
    point = lax.broadcasted_iota(jnp.int32, (1, WIDE), 1)
    e_lane = sum((point >= NODES * i).astype(jnp.int32) for i in range(1, PEERS + 1))
    inner = point - NODES * e_lane
    a_lane = sum((inner >= 6 * i).astype(jnp.int32) for i in range(1, 6))
    b_lane = inner - 6 * a_lane
    partner = jnp.full((1, WIDE), -1, jnp.int32)
    sides = jnp.zeros((1, WIDE), jnp.int32)
    for e in range(PEERS):
        prev = neigh[0, e] - first_elem
        nxt = neigh[1, e] - first_elem
        prev_here = (prev >= 0) & (prev < PEERS)
        next_here = (nxt >= 0) & (nxt < PEERS)
        head = head + jnp.where(prev_here, 0, e)
        tail = tail + jnp.where(next_here, 0, e)
        low = jnp.where(prev_here, prev * NODES + 5, -10000)
        high = jnp.where(next_here, nxt * NODES, -10000)
        here = e_lane == e
        partner = jnp.where(here & (b_lane == 0), low + 6 * a_lane, partner)
        partner = jnp.where(here & (b_lane == 5), high + 6 * a_lane, partner)
        sides = jnp.where(here, side[e], sides)
    for g in range(5):
        rows = lax.broadcasted_iota(jnp.int32, (128, WIDE), 0) + 128 * g
        perm[128 * g : 128 * g + 128, :] = jnp.where(rows == partner, 1.0, 0.0).astype(bf16)
    slot = sum((lane1 >= 6 * i).astype(jnp.int32) for i in range(1, 13))
    node = lane1 - 6 * slot
    head_node = jnp.where(slot < 12, head * NODES + 6 * node, -1)
    tail_node = jnp.where(slot < 12, tail * NODES + 6 * node + 5, -1)
    for g in range(5):
        rows = lax.broadcasted_iota(jnp.int32, (128, 128), 0) + 128 * g
        rims[128 * g : 128 * g + 128, 0:128] = jnp.where(rows == head_node, 1.0, 0.0).astype(bf16)
        rims[128 * g : 128 * g + 128, 128:256] = jnp.where(rows == tail_node, 1.0, 0.0).astype(bf16)
    line = lax.broadcasted_iota(jnp.int32, (128, WIDE), 0)
    line_slot = sum((line >= 6 * i).astype(jnp.int32) for i in range(1, 13))
    line_node = 6 * (line - 6 * line_slot)
    line_used = line_slot < 12
    for way, first in ((0, head * NODES), (1, tail * NODES + 5)):
        match = line_used & (point == first + line_node)
        rims_back[128 * way : 128 * way + 128, :] = jnp.where(match, 1.0, 0.0).astype(bf16)
    facing = (a_lane == 5 * sides) & (e_lane < PEERS)
    outward = (2 * sides - 1).astype(f32)
    face = jnp.where(facing, 15.0 * outward * geo[4] * geo[5], 0.0)
    order = lax.broadcasted_iota(jnp.int32, (OWN, 128), 0)
    pressure = jnp.zeros((OWN, 128), f32)
    for i in range(OWN):
        pressure = jnp.where(order == i, pres[i], pressure)
    for g in range(5):
        columns = slice(128 * g, 128 * g + 128)
        base[0, :, columns] = pressure * (face * geo[0])[:, columns]
        base[1, :, columns] = pressure * (face * geo[1])[:, columns]

    table_copy.wait()

    scratch = (even_odd, turns, grads, parts, hoops, sums)

    there1.forward(0, 6)

    @pl.when(half == 0)
    def _():
        pl.semaphore_wait(far, 2)
        there2.start()

    there1.forward(6, 8)

    @pl.when(half == 1)
    def _():
        pl.semaphore_wait(far, 2)
        there2.start()

    there1.arrive()

    evaluate(got1, result, own, shear, bulk, table, scratch)
    for i in range(PEERS):
        block = turn(result[OWN * i : OWN * i + OWN, :], 108)
        _, bottom = pack_rows(block, block)
        back0[i] = bottom
        back1[i] = block
    again0.start()
    home0[mode] = back0[mode]

    there2.arrive()
    for i in range(PEERS):
        state1[OWN * i : OWN * i + OWN, :] = turn(unpack_ragged(got1[OWN * i : OWN * i + OWN, :], got2[i]), 20)

    evaluate(state1, result, own, shear, bulk, table, scratch)
    for i in range(PEERS):
        back1[i] = jnp.where(lane < 108, result[OWN * i : OWN * i + OWN, :], back1[i])
    again1.start()
    home1[mode] = back1[mode]

    def side_by_side(pieces, c):
        columns = []
        for g in range(5):
            acc = jnp.zeros((OWN, 128), f32)
            for i in range(PEERS):
                low = max(NODES * i, 128 * g) - 128 * g
                high = min(NODES * i + NODES, 128 * g + 128) - 128 * g
                if low < high:
                    moved = turn(pieces[i], NODES * i - 128 * g - NODES * c)
                    acc = jnp.where((lane >= low) & (lane < high), moved, acc)
            columns.append(acc)
        whole = jnp.concatenate(columns, axis=1)
        return whole if c == 1 else whole + base[c // 2]

    def assemble(first, l_hi, l_lo, loaded):
        rows = slice(first, first + loaded.shape[0])
        partial[rows, :] = loaded + dot(l_hi, perm[...]) + dot(l_lo, perm[...])

    def trace(first, l_hi, l_lo):
        rows = slice(first, first + l_hi.shape[0])
        traces[rows, :] = dot(l_hi, rims[...]) + dot(l_lo, rims[...])

    again0.arrive()
    early = [turn(unpack_ragged(back1[i], home0[i]), 20) for i in range(PEERS)]
    early = jnp.concatenate([side_by_side(early, 1), side_by_side(early, 2)], axis=0)
    early_parts = split(early)
    trace(0, *early_parts)
    assemble(0, *early_parts, early)
    again1.arrive()
    late = [turn(unpack_ragged(home1[i], home0[i]), 20) for i in range(PEERS)]
    late = [side_by_side(late, 0)] + [side_by_side([home1[i] for i in range(PEERS)], c) for c in range(3)]
    late = jnp.concatenate(late, axis=0)
    late_parts = split(late)
    trace(64, *late_parts)

    for way in range(2):
        columns = slice(128 * way, 128 * way + 128)
        for s in range(2):
            tile = jnp.zeros((8, 128), f32)
            for t in range(12):
                tile = jnp.where(slot == t, traces[96 * s + 8 * t : 96 * s + 8 * t + 8, columns], tile)
            rim_out[way, 8 * s : 8 * s + 8, :] = tile

    to_prev = pltpu.make_async_remote_copy(
        src_ref=rim_out.at[0], dst_ref=rim_in.at[1], send_sem=rim_send.at[0], recv_sem=rim_recv.at[1],
        device_id=(jnp.maximum(elem - 1, 0), mode), device_id_type=MESH,
    )
    to_next = pltpu.make_async_remote_copy(
        src_ref=rim_out.at[1], dst_ref=rim_in.at[0], send_sem=rim_send.at[1], recv_sem=rim_recv.at[0],
        device_id=(jnp.minimum(elem + 1, runs - 1), mode), device_id_type=MESH,
    )

    @pl.when(elem > 0)
    def _():
        to_prev.start()

    @pl.when(elem < runs - 1)
    def _():
        to_next.start()

    assemble(64, *late_parts, late)

    @pl.when(elem > 0)
    def _():
        to_next.wait_recv()

    @pl.when(elem < runs - 1)
    def _():
        to_prev.wait_recv()

    arrived = []
    for way, there in ((0, elem > 0), (1, elem < runs - 1)):
        rows = []
        for s in range(2):
            tile = jnp.where(there, rim_in[way, 8 * s : 8 * s + 8, :], 0.0)
            rows += [jnp.where(slot == t, tile, 0.0) for t in range(12)]
        arrived.append(jnp.concatenate(rows, axis=0))
    a_hi, a_lo = split(jnp.concatenate(arrived, axis=1))
    places = [(0, 1), (0, 2), (0, 0), (1, 0), (1, 1), (1, 2)]
    for s in range(2):
        half_rows = slice(96 * s, 96 * s + 96)
        block = partial[half_rows, :] + dot(a_hi[half_rows], rims_back[...]) + dot(a_lo[half_rows], rims_back[...])
        for i in range(3):
            out[places[3 * s + i]] = block[32 * i : 32 * i + 32, 0:POINTS]
    for exchange in (there1, there2, again0, again1):
        exchange.finish()

    @pl.when(elem > 0)
    def _():
        to_prev.wait_send()

    @pl.when(elem < runs - 1)
    def _():
        to_next.wait_send()


EVALUATE_SCRATCH = [
    pltpu.VMEM((HALF, 256), f32),
    pltpu.VMEM((HALF, 256), f32),
    pltpu.VMEM((HALF, 768), f32),
    pltpu.VMEM((HALF, 1536), bf16),
    pltpu.VMEM((HALF, 512), f32),
    pltpu.VMEM((2 * ANGLES, 256), bf16),
]


def on_device(displacement, metric, weight_jac, radius, moduli, neighbours, inner_side, pressure):
    table = jnp.asarray(tables())
    hbm, vmem = pl.BlockSpec(memory_space=pltpu.HBM), pl.BlockSpec(memory_space=pltpu.VMEM)
    single = pltpu.SemaphoreType.DMA
    sems = [single, single, pltpu.SemaphoreType.DMA((len(CROSS),)), single] + [single] * 6
    return pl.pallas_call(
        kernel,
        out_shape=jax.ShapeDtypeStruct((2, 3, OWN, POINTS), f32),
        in_specs=[hbm] * 9,
        out_specs=vmem,
        scratch_shapes=[
            pltpu.VMEM((2, 3, OWN, POINTS), f32),
            pltpu.VMEM((4, POINTS), f32),
            pltpu.VMEM((POINTS,), f32),
            pltpu.VMEM((POINTS,), f32),
            pltpu.SMEM((2, PEERS), f32),
            pltpu.SMEM((2, PEERS), jnp.int32),
            pltpu.SMEM((PEERS,), jnp.int32),
            pltpu.SMEM((OWN,), f32),
            pltpu.VMEM((PEERS, 56, 128), f32),
            pltpu.VMEM((COEFS, 128), f32),
            pltpu.VMEM((PEERS, 24, 128), f32),
            pltpu.VMEM((COEFS, 128), f32),
            pltpu.VMEM((COEFS, 128), f32),
            pltpu.VMEM((PEERS, 24, 128), f32),
            pltpu.VMEM((PEERS, 32, 128), f32),
            pltpu.VMEM((PEERS, 24, 128), f32),
            pltpu.VMEM((PEERS, 32, 128), f32),
            pltpu.VMEM((WIDE, WIDE), bf16),
            pltpu.VMEM((WIDE, 256), bf16),
            pltpu.VMEM((256, WIDE), bf16),
            pltpu.VMEM((2, 16, 128), f32),
            pltpu.VMEM((2, 16, 128), f32),
            pltpu.VMEM((2, OWN, WIDE), f32),
            pltpu.VMEM((192, 256), f32),
            pltpu.VMEM((192, WIDE), f32),
            *EVALUATE_SCRATCH,
            pltpu.VMEM(table.shape, bf16),
            pltpu.VMEM((len(CROSS), 32, 128), f32),
            pltpu.SemaphoreType.DMA((2,)),
            pltpu.SemaphoreType.DMA((7,)),
            pltpu.SemaphoreType.DMA,
            *sems,
            pltpu.SemaphoreType.REGULAR,
            pltpu.SemaphoreType.DMA((2,)),
            pltpu.SemaphoreType.DMA((2,)),
        ],
        compiler_params=pltpu.CompilerParams(
            collective_id=0, has_side_effects=True, vmem_limit_bytes=64 * 2**20
        ),
        name="bellows",
    )(
        displacement, metric, weight_jac, radius, moduli, neighbours.T, inner_side, pressure,
        table,
    )


def solution(mesh):
    placed = (
        P(None, None, "mode", "elem"),
        P(None, "elem"),
        P("elem"),
        P("elem"),
        P(None, "elem"),
        P("elem", None),
        P("elem"),
        P("mode"),
    )
    return jax.shard_map(
        on_device,
        mesh=mesh,
        in_specs=placed,
        out_specs=P(None, None, "mode", "elem"),
        check_vma=False,
    )
```

```python
import math

import jax
import jax.numpy as jnp
import ml_dtypes
import numpy as np
from jax import lax
from jax.experimental import pallas as pl
from jax.experimental.pallas import tpu as pltpu
from jax.sharding import PartitionSpec as P

MODES = 256
ANGLES = 512
COEFS = 512
NODES = 36
PEERS = 16
OWN = 32
POINTS = 576
WIDE = 640
HALF = 272
STRIP = 16
MESH = pl.DeviceIdType.MESH
f32, bf16 = jnp.float32, jnp.bfloat16

LOCAL = [(dy, dc) for dy in (2, 1, 3, 0) for dc in (1, 0) if dy + dc]
CROSS = [(dy, dc, 1 - (dy + dc) % 2 * 2) for dy in (2, 1, 3, 0) for dc in (0, 1)]
LEG = 4


def line_derivative():
    inner_node = math.sqrt(1.0 / 3.0 - 2.0 * math.sqrt(7.0) / 21.0)
    outer_node = math.sqrt(1.0 / 3.0 + 2.0 * math.sqrt(7.0) / 21.0)
    gll_nodes = np.array([-1.0, -outer_node, -inner_node, inner_node, outer_node, 1.0])
    weights = np.array(
        [1.0 / np.prod([gll_nodes[j] - gll_nodes[k] for k in range(6) if k != j]) for j in range(6)]
    )
    derivative = np.zeros((6, 6))
    for i in range(6):
        for j in range(6):
            if i != j:
                derivative[i, j] = weights[j] / weights[i] / (gll_nodes[i] - gll_nodes[j])
        derivative[i, i] = -np.sum(derivative[i])
    return derivative


def halves(table):
    high = table.astype(np.float32).astype(ml_dtypes.bfloat16)
    low = (table - high.astype(np.float64)).astype(np.float32).astype(ml_dtypes.bfloat16)
    return high, low


def tables():
    counts = np.arange(HALF)
    orders = np.arange(MODES)
    phases = (counts[:, None] * orders[None, :] % ANGLES) * (2.0 * math.pi / ANGLES)
    used = (counts <= ANGLES // 2)[:, None]
    cosines, sines = np.cos(phases) * used, np.sin(phases) * used
    from_cos = np.concatenate([cosines, -orders * sines], axis=0)
    from_sin = np.concatenate([sines, orders * cosines], axis=0)
    step = 2.0 * math.pi / ANGLES
    ends = np.where(counts == 0, 0.5, 1.0)[: ANGLES // 2, None]
    cosines, sines = step * ends * cosines[: ANGLES // 2], step * sines[: ANGLES // 2]
    to_cos = np.concatenate([cosines, -orders * sines], axis=0).T
    to_sin = np.concatenate([sines, orders * cosines], axis=0).T
    derivative = line_derivative()
    slopes = [np.kron(derivative, np.eye(6)).T, np.kron(np.eye(6), derivative).T]
    spread = np.zeros((256, 768))
    for way, slope in enumerate(slopes):
        for c in range(3):
            column = 384 * way + 128 * c
            even, odd = NODES * c, 128 + NODES * c
            spread[even : even + NODES, column : column + 2 * NODES] = np.concatenate([slope, slope], axis=1)
            spread[odd : odd + NODES, column : column + 2 * NODES] = np.concatenate([slope, -slope], axis=1)
    blocks = [from_cos, from_sin, to_cos[:, 0:256], to_cos[:, 256:512], to_sin[:, 0:256], to_sin[:, 256:512]]
    blocks += [spread[:, 0:256], spread[:, 256:512], spread[:, 512:768], spread.T]
    return np.concatenate([part for block in blocks for part in halves(block)], axis=0)


BLOCK_ROWS = [2 * HALF] * 2 + [256] * 4 + [256] * 3 + [768]
BLOCK_START = np.concatenate([[0], np.cumsum([2 * n for n in BLOCK_ROWS])]).tolist()


def split(values):
    high = values.astype(bf16)
    return high, (values - high.astype(f32)).astype(bf16)


def dot(a, b):
    return jnp.dot(a, b, preferred_element_type=f32)


def turn(values, shift):
    shift = shift % 128
    return pltpu.roll(values, shift, 1) if shift else values


def evaluate(coefs, result, rows, shear, bulk, table, scratch):
    def block(i):
        first, count = BLOCK_START[i], BLOCK_ROWS[i]
        return table[first : first + count, :], table[first + count : first + 2 * count, :]

    even_odd, turns, grads, parts, hoops, sums = scratch
    xi_r, xi_z, eta_r, eta_z, weight, radius = rows
    rho = 1.0 / radius
    scale = weight * radius
    back = [scale * xi_r, scale * xi_z, scale * eta_r, scale * eta_z]
    lane = lax.broadcasted_iota(jnp.int32, (STRIP, 128), 1)
    plus = lane < NODES

    def product(high, low, a_hi, a_lo):
        both = dot(high, jnp.concatenate([a_hi, a_lo], axis=1))
        return both[:, 0:128] + both[:, 128:256] + dot(low, a_hi)

    for order in range(2):
        both = product(*block(order), *split(coefs[pl.ds(order, MODES, stride=2), :]))
        even_odd[:, 128 * order : 128 * order + 128] = both[0:HALF]
        turns[:, 128 * order : 128 * order + 128] = both[HALF : 2 * HALF]
    sign = 1.0 - 2.0 * (lax.broadcasted_iota(jnp.int32, (HALF, 128), 0) % 2).astype(f32)
    even_odd[:, 0:128] = even_odd[:, 0:128] + sign * coefs[1:2, :]

    high, low = split(even_odd[...])
    for i in range(3):
        b_hi, b_lo = block(6 + i)
        grads[:, 256 * i : 256 * i + 256] = dot(high, b_hi) + dot(low, b_hi) + dot(high, b_lo)

    def strip(k, _):
        here = pl.ds(pl.multiple_of(k * STRIP, STRIP), STRIP)
        even, odd = even_odd[here, 0:128], even_odd[here, 128:256]
        turned_odd, turned_even = turns[here, 0:128], turns[here, 128:256]
        u_plus, u_minus = even + odd, even - odd
        r_plus, r_minus = turned_even + turned_odd, turned_even - turned_odd
        v = [None] * 9
        for c in range(3):
            ax = grads[here, 128 * c : 128 * c + 128]
            ae = grads[here, 384 + 128 * c : 512 + 128 * c]
            v[c] = xi_r * ax + eta_r * ae
            v[3 + c] = xi_z * ax + eta_z * ae
        v[6] = jnp.where(plus, r_plus - turn(u_plus, -NODES), turn(r_minus, NODES) - u_minus)
        v[7] = jnp.where(plus, turn(r_plus, -NODES) + u_plus, r_minus + turn(u_minus, NODES))
        v[8] = jnp.where(plus, turn(r_plus, -2 * NODES), turn(r_minus, -NODES))
        deform = [
            [1.0 + v[0], rho * v[6], v[3]],
            [v[1], 1.0 + rho * v[7], v[4]],
            [v[2], rho * v[8], 1.0 + v[5]],
        ]
        cof = [
            [
                deform[(i + 1) % 3][(j + 1) % 3] * deform[(i + 2) % 3][(j + 2) % 3]
                - deform[(i + 1) % 3][(j + 2) % 3] * deform[(i + 2) % 3][(j + 1) % 3]
                for j in range(3)
            ]
            for i in range(3)
        ]
        volume = deform[0][0] * cof[0][0] + deform[0][1] * cof[0][1] + deform[0][2] * cof[0][2]
        factor = bulk * (volume - 1.0) - shear
        piola = [[shear * deform[i][j] + factor * cof[i][j] for j in range(3)] for i in range(3)]
        for c in range(3):
            for i, value in (
                (c, back[0] * piola[c][0] + back[1] * piola[c][2]),
                (3 + c, back[2] * piola[c][0] + back[3] * piola[c][2]),
            ):
                v_hi, v_lo = split(value)
                parts[here, 128 * i : 128 * i + 128] = v_hi
                parts[here, 768 + 128 * i : 896 + 128 * i] = v_lo
        hoop = [weight * piola[c][1] for c in range(3)]
        for i, sense in ((0, 1.0), (1, -1.0)):
            pair = [jnp.where(plus, h + sense * turn(h, -NODES), 0.0) for h in hoop]
            first = 256 * i
            hoops[here, first : first + 128] = pair[1] - turn(pair[0], NODES)
            hoops[here, first + 128 : first + 256] = (
                pair[0] + turn(pair[1], NODES) + turn(pair[2], 2 * NODES)
            )
        return 0

    lax.fori_loop(0, HALF // STRIP, strip, 0, unroll=True)

    high, low = parts[:, 0:768], parts[:, 768:1536]
    b_hi, b_lo = block(9)
    straight = dot(high, b_hi) + dot(low, b_hi) + dot(high, b_lo)
    even = straight[:, 0:128] + hoops[:, 0:128]
    odd = straight[:, 128:256] + hoops[:, 256:384]
    half = ANGLES // 2
    for i, value in enumerate((even, hoops[:, 384:512], odd, hoops[:, 128:256])):
        v_hi, v_lo = split(value[0:half])
        sums[half * i : half * i + half, 0:128] = v_hi
        sums[half * i : half * i + half, 128:256] = v_lo

    step = 2.0 * math.pi / ANGLES
    row = lax.broadcasted_iota(jnp.int32, (MODES, 128), 0)
    signed = (0.5 * step) * (1.0 - 2.0 * (row % 2).astype(f32))
    weights = jnp.where(row == 0, 0.5 * signed, signed) * 2.0
    last = jnp.sum(weights * even[0:half], axis=0, keepdims=True) + 0.5 * step * even[half : half + 1]
    pieces = [(sums[half * i : half * i + half, 0:128], sums[half * i : half * i + half, 128:256]) for i in range(4)]
    cos_part = product(*block(2), *pieces[0]) + product(*block(3), *pieces[1])
    result[pl.ds(0, MODES, stride=2), :] = cos_part + signed * even[half : half + 1]
    sin_part = product(*block(4), *pieces[2]) + product(*block(5), *pieces[3])
    sin_part = sin_part + (row.astype(f32) * signed) * hoops[half : half + 1, 128:256]
    result[pl.ds(1, MODES, stride=2), :] = jnp.where(row == 0, last, sin_part)


def kernel(
    disp_in, metric_in, weight_in, radius_in, moduli_in, neigh_in, side_in, pres_in,
    table_in,
    out,
    disp, metric, weights, radii, moduli, neigh, side, pres,
    pack, got1, got2, state1, result, back0, back1, home0, home1, perm, rims, rims_back, rim_out, rim_in, base, traces, partial,
    even_odd, turns, grads, parts, hoops, sums,
    table,
    relay1,
    disp_sem, small_sem, table_sem,
    s1, r1, m1, o1, s2, r2, s3, r3, s4, r4, far,
    rim_send, rim_recv,
):
    sems1, sems2, sems3, sems4 = (s1, r1, m1, o1), (s2, r2, None, None), (s3, r3, None, None), (s4, r4, None, None)
    elem = lax.axis_index("elem")
    mode = lax.axis_index("mode")
    runs = lax.axis_size("elem")
    half, rest = mode // 8, mode % 8
    row, core = rest // 2, rest % 2
    height = half * 8 + elem // 4

    def place(dz, dy, dc):
        there = (height + dz + 16) % 16
        column = (row + dy + 4) % 4 * 2 + (core + dc + 2) % 2
        return there % 8 * 4 + elem % 4, there // 8 * 8 + column

    disp_copies = [pltpu.make_async_copy(disp_in.at[s], disp.at[s], disp_sem.at[s]) for s in range(2)]
    for copy in disp_copies:
        copy.start()
    barrier = pltpu.get_barrier_semaphore()
    senders = [place(-LEG * up, -dy, -dc) for dy, dc, up in CROSS] + [place(LEG, 0, 0)]
    senders += [place(0, -dy, -dc) for dy, dc in LOCAL]
    for sender in senders:
        pl.semaphore_signal(barrier, inc=1, device_id=sender, device_id_type=MESH)

    @pl.when(elem > 0)
    def _():
        pl.semaphore_signal(barrier, inc=1, device_id=(elem - 1, mode), device_id_type=MESH)

    @pl.when(elem < runs - 1)
    def _():
        pl.semaphore_signal(barrier, inc=1, device_id=(elem + 1, mode), device_id_type=MESH)

    small_copies = [
        pltpu.make_async_copy(src, dst, small_sem.at[i])
        for i, (src, dst) in enumerate(
            [(metric_in, metric), (weight_in, weights), (radius_in, radii), (moduli_in, moduli),
             (neigh_in, neigh), (side_in, side), (pres_in, pres)]
        )
    ]
    for copy in small_copies:
        copy.start()

    lane = lax.broadcasted_iota(jnp.int32, (OWN, 128), 1)
    lane8 = lax.broadcasted_iota(jnp.int32, (8, 128), 1)

    def column(s, c, g):
        if g < 4:
            return disp[s, c, :, 128 * g : 128 * g + 128]
        return jnp.concatenate([disp[s, c, :, 512:576], jnp.zeros((OWN, 64), f32)], axis=1)

    def gather_element(s, j, base_lane):
        result = jnp.zeros((OWN, 128), f32)
        for c in range(3):
            target = NODES * c + base_lane
            first = NODES * j
            for g in range(first // 128, (first + NODES - 1) // 128 + 1):
                low = max(first, 128 * g)
                high = min(first + NODES, 128 * g + 128)
                moved = turn(column(s, c, g), target - (first - 128 * g))
                begin = (target + low - first) % 128
                end = begin + high - low
                inside = (lane >= begin) & (lane < end)
                if end > 128:
                    inside = (lane >= begin) | (lane < end - 128)
                result = jnp.where(inside, moved, result)
        return result

    def pack_rows(full, ragged):
        last = ragged[24:32]
        tails = [turn(last, 88), turn(last, 48), turn(last, 8)]
        rows = [jnp.where(lane8 < 88, ragged[8 * t : 8 * t + 8], tails[t]) for t in range(3)]
        return jnp.where(lane < 108, full, ragged), jnp.concatenate(rows, axis=0)

    def unpack_ragged(first, second):
        rows = [
            jnp.where(lane8 < 88, second[8 * t : 8 * t + 8], first[8 * t : 8 * t + 8]) for t in range(3)
        ]
        moved = [turn(second[0:8], -88), turn(second[8:16], -48), turn(second[16:24], -8)]
        last = jnp.where(lane8 < 40, moved[0], jnp.where(lane8 < 80, moved[1], moved[2]))
        rows.append(jnp.where(lane8 < 88, last, first[24:32]))
        return jnp.concatenate(rows, axis=0)

    for copy in disp_copies:
        copy.wait()
    for j in range(PEERS):
        full = gather_element(0, j, 0)
        ragged = gather_element(1, j, 108)
        top, bottom = pack_rows(full, ragged)
        pack[j, 0:32, :] = top
        pack[j, 32:56, :] = bottom

    table_copy = pltpu.make_async_copy(table_in, table, table_sem)
    table_copy.start()

    neighbours_there = 2 - (elem == 0).astype(jnp.int32) - (elem == runs - 1).astype(jnp.int32)
    pl.semaphore_wait(barrier, len(senders) + neighbours_there)

    class Exchange:
        def __init__(self, source, target, arrivals, sems, relay=None):
            send, recv, relayed, onward = sems
            self.all = arrivals, relay, send, recv, onward
            self.first, self.second = [], []

            def copy(src, dst, sent, received, to):
                return pltpu.make_async_remote_copy(
                    src_ref=src, dst_ref=dst, send_sem=sent, recv_sem=received,
                    device_id=to, device_id_type=MESH,
                )

            for i, (dy, dc, up) in enumerate(CROSS):
                owner = place(2 * LEG, dy, dc)
                if relay is None:
                    self.first.append(copy(source(owner[1]), target(mode), send, recv, owner))
                    continue
                origin = place(-LEG * up, 0, 0)[1]
                self.first.append(copy(source(owner[1]), relay.at[i], send, relayed.at[i], place(LEG * up, 0, 0)))
                self.second.append(copy(relay.at[i], target(origin), onward, recv, place(LEG * up, dy, dc)))
            for dy, dc in LOCAL:
                to = place(0, dy, dc)
                self.first.append(copy(source(to[1]), target(mode), send, recv, to))

        def start(self):
            for one in self.first:
                one.start()

        def forward(self, low=0, high=8):
            for first, second in zip(self.first[low:high], self.second[low:high]):
                first.wait_recv()
                second.start()

        def arrive(self):
            arrivals, _, _, recv, _ = self.all
            pltpu.make_async_copy(arrivals, arrivals, recv).wait()

        def finish(self):
            arrivals, relay, send, _, onward = self.all
            pltpu.make_async_copy(arrivals, arrivals, send).wait()
            if relay is not None:
                pltpu.make_async_copy(relay, relay, onward).wait()

    def full_rows(me):
        return got1.at[pl.ds(pl.multiple_of(me * OWN, OWN), OWN)]

    there1 = Exchange(lambda to: pack.at[to, 0:32], full_rows, got1.at[0 : 15 * OWN], sems1, relay1)
    there2 = Exchange(lambda to: pack.at[to, 32:56], lambda me: got2.at[me], got2.at[0:15], sems2)
    again0 = Exchange(lambda to: back0.at[to], lambda me: home0.at[me], home0.at[0:15], sems3)
    again1 = Exchange(lambda to: back1.at[to], lambda me: home1.at[me], home1.at[0:15], sems4)
    there1.start()
    for dz in (LEG, -LEG):
        pl.semaphore_signal(far, inc=1, device_id=place(dz, 0, 0), device_id_type=MESH)
    got1[pl.ds(pl.multiple_of(mode * OWN, OWN), OWN), :] = pack[mode, 0:32, :]
    got2[mode] = pack[mode, 32:56, :]

    for copy in small_copies:
        copy.wait()

    def wide(pieces):
        return jnp.concatenate(pieces + [jnp.zeros((1, WIDE - POINTS), f32)], axis=1)

    def as_row(ref):
        return wide([ref[128 * g : min(128 * g + 128, POINTS)].reshape(1, -1) for g in range(5)])

    geo = [wide([metric[i : i + 1, :]]) for i in range(4)] + [as_row(weights), as_row(radii)]
    stacked = jnp.concatenate(geo + [jnp.zeros((2, WIDE), f32)], axis=0)
    stacked = pltpu.roll(stacked, (WIDE - NODES * mode) % WIDE, 1)

    def own_row(i):
        return stacked[i : i + 1, 0:128]

    lane1 = lax.broadcasted_iota(jnp.int32, (1, 128), 1)
    own = [jnp.where(lane1 < NODES, own_row(i), 0.0) for i in range(6)]
    own = [r + turn(r, NODES) for r in own]
    own[5] = jnp.where(lane1 < 2 * NODES, own[5], 1.0)
    shear = moduli[0, mode]
    bulk = moduli[1, mode]

    first_elem = elem * PEERS
    head = jnp.int32(0)
    tail = jnp.int32(0)
    point = lax.broadcasted_iota(jnp.int32, (1, WIDE), 1)
    e_lane = sum((point >= NODES * i).astype(jnp.int32) for i in range(1, PEERS + 1))
    inner = point - NODES * e_lane
    a_lane = sum((inner >= 6 * i).astype(jnp.int32) for i in range(1, 6))
    b_lane = inner - 6 * a_lane
    partner = jnp.full((1, WIDE), -1, jnp.int32)
    sides = jnp.zeros((1, WIDE), jnp.int32)
    for e in range(PEERS):
        prev = neigh[0, e] - first_elem
        nxt = neigh[1, e] - first_elem
        prev_here = (prev >= 0) & (prev < PEERS)
        next_here = (nxt >= 0) & (nxt < PEERS)
        head = head + jnp.where(prev_here, 0, e)
        tail = tail + jnp.where(next_here, 0, e)
        low = jnp.where(prev_here, prev * NODES + 5, -10000)
        high = jnp.where(next_here, nxt * NODES, -10000)
        here = e_lane == e
        partner = jnp.where(here & (b_lane == 0), low + 6 * a_lane, partner)
        partner = jnp.where(here & (b_lane == 5), high + 6 * a_lane, partner)
        sides = jnp.where(here, side[e], sides)
    for g in range(5):
        rows = lax.broadcasted_iota(jnp.int32, (128, WIDE), 0) + 128 * g
        perm[128 * g : 128 * g + 128, :] = jnp.where(rows == partner, 1.0, 0.0).astype(bf16)
    slot = sum((lane1 >= 6 * i).astype(jnp.int32) for i in range(1, 13))
    node = lane1 - 6 * slot
    head_node = jnp.where(slot < 12, head * NODES + 6 * node, -1)
    tail_node = jnp.where(slot < 12, tail * NODES + 6 * node + 5, -1)
    for g in range(5):
        rows = lax.broadcasted_iota(jnp.int32, (128, 128), 0) + 128 * g
        rims[128 * g : 128 * g + 128, 0:128] = jnp.where(rows == head_node, 1.0, 0.0).astype(bf16)
        rims[128 * g : 128 * g + 128, 128:256] = jnp.where(rows == tail_node, 1.0, 0.0).astype(bf16)
    line = lax.broadcasted_iota(jnp.int32, (128, WIDE), 0)
    line_slot = sum((line >= 6 * i).astype(jnp.int32) for i in range(1, 13))
    line_node = 6 * (line - 6 * line_slot)
    line_used = line_slot < 12
    for way, first in ((0, head * NODES), (1, tail * NODES + 5)):
        match = line_used & (point == first + line_node)
        rims_back[128 * way : 128 * way + 128, :] = jnp.where(match, 1.0, 0.0).astype(bf16)
    facing = (a_lane == 5 * sides) & (e_lane < PEERS)
    outward = (2 * sides - 1).astype(f32)
    face = jnp.where(facing, 15.0 * outward * geo[4] * geo[5], 0.0)
    order = lax.broadcasted_iota(jnp.int32, (OWN, 128), 0)
    pressure = jnp.zeros((OWN, 128), f32)
    for i in range(OWN):
        pressure = jnp.where(order == i, pres[i], pressure)
    for g in range(5):
        columns = slice(128 * g, 128 * g + 128)
        base[0, :, columns] = pressure * (face * geo[0])[:, columns]
        base[1, :, columns] = pressure * (face * geo[1])[:, columns]

    table_copy.wait()

    scratch = (even_odd, turns, grads, parts, hoops, sums)

    there1.forward(0, 7)

    @pl.when(half == 0)
    def _():
        pl.semaphore_wait(far, 2)
        there2.start()

    there1.forward(7, 8)

    @pl.when(half == 1)
    def _():
        pl.semaphore_wait(far, 2)
        there2.start()

    there1.arrive()

    evaluate(got1, result, own, shear, bulk, table, scratch)
    for i in range(PEERS):
        block = turn(result[OWN * i : OWN * i + OWN, :], 108)
        _, bottom = pack_rows(block, block)
        back0[i] = bottom
        back1[i] = block
    again0.start()
    home0[mode] = back0[mode]

    there2.arrive()
    for i in range(PEERS):
        state1[OWN * i : OWN * i + OWN, :] = turn(unpack_ragged(got1[OWN * i : OWN * i + OWN, :], got2[i]), 20)

    evaluate(state1, result, own, shear, bulk, table, scratch)
    for i in range(PEERS):
        back1[i] = jnp.where(lane < 108, result[OWN * i : OWN * i + OWN, :], back1[i])
    again1.start()
    home1[mode] = back1[mode]

    def side_by_side(pieces, c):
        columns = []
        for g in range(5):
            acc = jnp.zeros((OWN, 128), f32)
            for i in range(PEERS):
                low = max(NODES * i, 128 * g) - 128 * g
                high = min(NODES * i + NODES, 128 * g + 128) - 128 * g
                if low < high:
                    moved = turn(pieces[i], NODES * i - 128 * g - NODES * c)
                    acc = jnp.where((lane >= low) & (lane < high), moved, acc)
            columns.append(acc)
        whole = jnp.concatenate(columns, axis=1)
        return whole if c == 1 else whole + base[c // 2]

    def assemble(first, l_hi, l_lo, loaded):
        rows = slice(first, first + loaded.shape[0])
        partial[rows, :] = loaded + dot(l_hi, perm[...]) + dot(l_lo, perm[...])

    def trace(first, l_hi, l_lo):
        rows = slice(first, first + l_hi.shape[0])
        traces[rows, :] = dot(l_hi, rims[...]) + dot(l_lo, rims[...])

    again0.arrive()
    early = [turn(unpack_ragged(back1[i], home0[i]), 20) for i in range(PEERS)]
    early = jnp.concatenate([side_by_side(early, 1), side_by_side(early, 2)], axis=0)
    early_parts = split(early)
    trace(0, *early_parts)
    assemble(0, *early_parts, early)
    again1.arrive()
    late = [turn(unpack_ragged(home1[i], home0[i]), 20) for i in range(PEERS)]
    late = [side_by_side(late, 0)] + [side_by_side([home1[i] for i in range(PEERS)], c) for c in range(3)]
    late = jnp.concatenate(late, axis=0)
    late_parts = split(late)
    trace(64, *late_parts)

    for way in range(2):
        columns = slice(128 * way, 128 * way + 128)
        for s in range(2):
            tile = jnp.zeros((8, 128), f32)
            for t in range(12):
                tile = jnp.where(slot == t, traces[96 * s + 8 * t : 96 * s + 8 * t + 8, columns], tile)
            rim_out[way, 8 * s : 8 * s + 8, :] = tile

    to_prev = pltpu.make_async_remote_copy(
        src_ref=rim_out.at[0], dst_ref=rim_in.at[1], send_sem=rim_send.at[0], recv_sem=rim_recv.at[1],
        device_id=(jnp.maximum(elem - 1, 0), mode), device_id_type=MESH,
    )
    to_next = pltpu.make_async_remote_copy(
        src_ref=rim_out.at[1], dst_ref=rim_in.at[0], send_sem=rim_send.at[1], recv_sem=rim_recv.at[0],
        device_id=(jnp.minimum(elem + 1, runs - 1), mode), device_id_type=MESH,
    )

    @pl.when(elem > 0)
    def _():
        to_prev.start()

    @pl.when(elem < runs - 1)
    def _():
        to_next.start()

    assemble(64, *late_parts, late)

    @pl.when(elem > 0)
    def _():
        to_next.wait_recv()

    @pl.when(elem < runs - 1)
    def _():
        to_prev.wait_recv()

    arrived = []
    for way, there in ((0, elem > 0), (1, elem < runs - 1)):
        rows = []
        for s in range(2):
            tile = jnp.where(there, rim_in[way, 8 * s : 8 * s + 8, :], 0.0)
            rows += [jnp.where(slot == t, tile, 0.0) for t in range(12)]
        arrived.append(jnp.concatenate(rows, axis=0))
    a_hi, a_lo = split(jnp.concatenate(arrived, axis=1))
    places = [(0, 1), (0, 2), (0, 0), (1, 0), (1, 1), (1, 2)]
    for s in range(2):
        half_rows = slice(96 * s, 96 * s + 96)
        block = partial[half_rows, :] + dot(a_hi[half_rows], rims_back[...]) + dot(a_lo[half_rows], rims_back[...])
        for i in range(3):
            out[places[3 * s + i]] = block[32 * i : 32 * i + 32, 0:POINTS]
    for exchange in (there1, there2, again0, again1):
        exchange.finish()

    @pl.when(elem > 0)
    def _():
        to_prev.wait_send()

    @pl.when(elem < runs - 1)
    def _():
        to_next.wait_send()


EVALUATE_SCRATCH = [
    pltpu.VMEM((HALF, 256), f32),
    pltpu.VMEM((HALF, 256), f32),
    pltpu.VMEM((HALF, 768), f32),
    pltpu.VMEM((HALF, 1536), bf16),
    pltpu.VMEM((HALF, 512), f32),
    pltpu.VMEM((2 * ANGLES, 256), bf16),
]


def on_device(displacement, metric, weight_jac, radius, moduli, neighbours, inner_side, pressure):
    table = jnp.asarray(tables())
    hbm, vmem = pl.BlockSpec(memory_space=pltpu.HBM), pl.BlockSpec(memory_space=pltpu.VMEM)
    single = pltpu.SemaphoreType.DMA
    sems = [single, single, pltpu.SemaphoreType.DMA((len(CROSS),)), single] + [single] * 6
    return pl.pallas_call(
        kernel,
        out_shape=jax.ShapeDtypeStruct((2, 3, OWN, POINTS), f32),
        in_specs=[hbm] * 9,
        out_specs=vmem,
        scratch_shapes=[
            pltpu.VMEM((2, 3, OWN, POINTS), f32),
            pltpu.VMEM((4, POINTS), f32),
            pltpu.VMEM((POINTS,), f32),
            pltpu.VMEM((POINTS,), f32),
            pltpu.SMEM((2, PEERS), f32),
            pltpu.SMEM((2, PEERS), jnp.int32),
            pltpu.SMEM((PEERS,), jnp.int32),
            pltpu.SMEM((OWN,), f32),
            pltpu.VMEM((PEERS, 56, 128), f32),
            pltpu.VMEM((COEFS, 128), f32),
            pltpu.VMEM((PEERS, 24, 128), f32),
            pltpu.VMEM((COEFS, 128), f32),
            pltpu.VMEM((COEFS, 128), f32),
            pltpu.VMEM((PEERS, 24, 128), f32),
            pltpu.VMEM((PEERS, 32, 128), f32),
            pltpu.VMEM((PEERS, 24, 128), f32),
            pltpu.VMEM((PEERS, 32, 128), f32),
            pltpu.VMEM((WIDE, WIDE), bf16),
            pltpu.VMEM((WIDE, 256), bf16),
            pltpu.VMEM((256, WIDE), bf16),
            pltpu.VMEM((2, 16, 128), f32),
            pltpu.VMEM((2, 16, 128), f32),
            pltpu.VMEM((2, OWN, WIDE), f32),
            pltpu.VMEM((192, 256), f32),
            pltpu.VMEM((192, WIDE), f32),
            *EVALUATE_SCRATCH,
            pltpu.VMEM(table.shape, bf16),
            pltpu.VMEM((len(CROSS), 32, 128), f32),
            pltpu.SemaphoreType.DMA((2,)),
            pltpu.SemaphoreType.DMA((7,)),
            pltpu.SemaphoreType.DMA,
            *sems,
            pltpu.SemaphoreType.REGULAR,
            pltpu.SemaphoreType.DMA((2,)),
            pltpu.SemaphoreType.DMA((2,)),
        ],
        compiler_params=pltpu.CompilerParams(
            collective_id=0, has_side_effects=True, vmem_limit_bytes=64 * 2**20
        ),
        name="bellows",
    )(
        displacement, metric, weight_jac, radius, moduli, neighbours.T, inner_side, pressure,
        table,
    )


def solution(mesh):
    placed = (
        P(None, None, "mode", "elem"),
        P(None, "elem"),
        P("elem"),
        P("elem"),
        P(None, "elem"),
        P("elem", None),
        P("elem"),
        P("mode"),
    )
    return jax.shard_map(
        on_device,
        mesh=mesh,
        in_specs=placed,
        out_specs=P(None, None, "mode", "elem"),
        check_vma=False,
    )
```

```python
import math

import jax
import jax.numpy as jnp
import ml_dtypes
import numpy as np
from jax import lax
from jax.experimental import pallas as pl
from jax.experimental.pallas import tpu as pltpu
from jax.sharding import PartitionSpec as P

MODES = 256
ANGLES = 512
COEFS = 512
NODES = 36
PEERS = 16
OWN = 32
POINTS = 576
WIDE = 640
HALF = 272
STRIP = 16
MESH = pl.DeviceIdType.MESH
f32, bf16 = jnp.float32, jnp.bfloat16

LOCAL = [(dy, dc) for dy in (2, 1, 3, 0) for dc in (1, 0) if dy + dc]
CROSS = [(dy, dc, 1 - (dy + dc) % 2 * 2) for dy in (2, 1, 3, 0) for dc in (0, 1)]
LEG = 4


def line_derivative():
    inner_node = math.sqrt(1.0 / 3.0 - 2.0 * math.sqrt(7.0) / 21.0)
    outer_node = math.sqrt(1.0 / 3.0 + 2.0 * math.sqrt(7.0) / 21.0)
    gll_nodes = np.array([-1.0, -outer_node, -inner_node, inner_node, outer_node, 1.0])
    weights = np.array(
        [1.0 / np.prod([gll_nodes[j] - gll_nodes[k] for k in range(6) if k != j]) for j in range(6)]
    )
    derivative = np.zeros((6, 6))
    for i in range(6):
        for j in range(6):
            if i != j:
                derivative[i, j] = weights[j] / weights[i] / (gll_nodes[i] - gll_nodes[j])
        derivative[i, i] = -np.sum(derivative[i])
    return derivative


def halves(table):
    high = table.astype(np.float32).astype(ml_dtypes.bfloat16)
    low = (table - high.astype(np.float64)).astype(np.float32).astype(ml_dtypes.bfloat16)
    return high, low


def tables():
    counts = np.arange(HALF)
    orders = np.arange(MODES)
    phases = (counts[:, None] * orders[None, :] % ANGLES) * (2.0 * math.pi / ANGLES)
    used = (counts <= ANGLES // 2)[:, None]
    cosines, sines = np.cos(phases) * used, np.sin(phases) * used
    from_cos = np.concatenate([cosines, -orders * sines], axis=0)
    from_sin = np.concatenate([sines, orders * cosines], axis=0)
    step = 2.0 * math.pi / ANGLES
    ends = np.where(counts == 0, 0.5, 1.0)[: ANGLES // 2, None]
    cosines, sines = step * ends * cosines[: ANGLES // 2], step * sines[: ANGLES // 2]
    to_cos = np.concatenate([cosines, -orders * sines], axis=0).T
    to_sin = np.concatenate([sines, orders * cosines], axis=0).T
    derivative = line_derivative()
    slopes = [np.kron(derivative, np.eye(6)).T, np.kron(np.eye(6), derivative).T]
    spread = np.zeros((256, 768))
    for way, slope in enumerate(slopes):
        for c in range(3):
            column = 384 * way + 128 * c
            even, odd = NODES * c, 128 + NODES * c
            spread[even : even + NODES, column : column + 2 * NODES] = np.concatenate([slope, slope], axis=1)
            spread[odd : odd + NODES, column : column + 2 * NODES] = np.concatenate([slope, -slope], axis=1)
    blocks = [from_cos, from_sin, to_cos[:, 0:256], to_cos[:, 256:512], to_sin[:, 0:256], to_sin[:, 256:512]]
    blocks += [spread[:, 0:256], spread[:, 256:512], spread[:, 512:768], spread.T]
    return np.concatenate([part for block in blocks for part in halves(block)], axis=0)


BLOCK_ROWS = [2 * HALF] * 2 + [256] * 4 + [256] * 3 + [768]
BLOCK_START = np.concatenate([[0], np.cumsum([2 * n for n in BLOCK_ROWS])]).tolist()


def split(values):
    high = values.astype(bf16)
    return high, (values - high.astype(f32)).astype(bf16)


def dot(a, b):
    return jnp.dot(a, b, preferred_element_type=f32)


def turn(values, shift):
    shift = shift % 128
    return pltpu.roll(values, shift, 1) if shift else values


def evaluate(coefs, result, rows, shear, bulk, table, scratch):
    def block(i):
        first, count = BLOCK_START[i], BLOCK_ROWS[i]
        return table[first : first + count, :], table[first + count : first + 2 * count, :]

    even_odd, turns, grads, parts, hoops, sums = scratch
    xi_r, xi_z, eta_r, eta_z, weight, radius = rows
    rho = 1.0 / radius
    scale = weight * radius
    back = [scale * xi_r, scale * xi_z, scale * eta_r, scale * eta_z]
    lane = lax.broadcasted_iota(jnp.int32, (STRIP, 128), 1)
    plus = lane < NODES

    def product(high, low, a_hi, a_lo):
        both = dot(high, jnp.concatenate([a_hi, a_lo], axis=1))
        return both[:, 0:128] + both[:, 128:256] + dot(low, a_hi)

    for order in range(2):
        both = product(*block(order), *split(coefs[pl.ds(order, MODES, stride=2), :]))
        even_odd[:, 128 * order : 128 * order + 128] = both[0:HALF]
        turns[:, 128 * order : 128 * order + 128] = both[HALF : 2 * HALF]
    sign = 1.0 - 2.0 * (lax.broadcasted_iota(jnp.int32, (HALF, 128), 0) % 2).astype(f32)
    even_odd[:, 0:128] = even_odd[:, 0:128] + sign * coefs[1:2, :]

    high, low = split(even_odd[...])
    for i in range(3):
        b_hi, b_lo = block(6 + i)
        grads[:, 256 * i : 256 * i + 256] = dot(high, b_hi) + dot(low, b_hi) + dot(high, b_lo)

    def strip(k, _):
        here = pl.ds(pl.multiple_of(k * STRIP, STRIP), STRIP)
        even, odd = even_odd[here, 0:128], even_odd[here, 128:256]
        turned_odd, turned_even = turns[here, 0:128], turns[here, 128:256]
        u_plus, u_minus = even + odd, even - odd
        r_plus, r_minus = turned_even + turned_odd, turned_even - turned_odd
        v = [None] * 9
        for c in range(3):
            ax = grads[here, 128 * c : 128 * c + 128]
            ae = grads[here, 384 + 128 * c : 512 + 128 * c]
            v[c] = xi_r * ax + eta_r * ae
            v[3 + c] = xi_z * ax + eta_z * ae
        v[6] = jnp.where(plus, r_plus - turn(u_plus, -NODES), turn(r_minus, NODES) - u_minus)
        v[7] = jnp.where(plus, turn(r_plus, -NODES) + u_plus, r_minus + turn(u_minus, NODES))
        v[8] = jnp.where(plus, turn(r_plus, -2 * NODES), turn(r_minus, -NODES))
        deform = [
            [1.0 + v[0], rho * v[6], v[3]],
            [v[1], 1.0 + rho * v[7], v[4]],
            [v[2], rho * v[8], 1.0 + v[5]],
        ]
        cof = [
            [
                deform[(i + 1) % 3][(j + 1) % 3] * deform[(i + 2) % 3][(j + 2) % 3]
                - deform[(i + 1) % 3][(j + 2) % 3] * deform[(i + 2) % 3][(j + 1) % 3]
                for j in range(3)
            ]
            for i in range(3)
        ]
        volume = deform[0][0] * cof[0][0] + deform[0][1] * cof[0][1] + deform[0][2] * cof[0][2]
        factor = bulk * (volume - 1.0) - shear
        piola = [[shear * deform[i][j] + factor * cof[i][j] for j in range(3)] for i in range(3)]
        for c in range(3):
            for i, value in (
                (c, back[0] * piola[c][0] + back[1] * piola[c][2]),
                (3 + c, back[2] * piola[c][0] + back[3] * piola[c][2]),
            ):
                v_hi, v_lo = split(value)
                parts[here, 128 * i : 128 * i + 128] = v_hi
                parts[here, 768 + 128 * i : 896 + 128 * i] = v_lo
        hoop = [weight * piola[c][1] for c in range(3)]
        for i, sense in ((0, 1.0), (1, -1.0)):
            pair = [jnp.where(plus, h + sense * turn(h, -NODES), 0.0) for h in hoop]
            first = 256 * i
            hoops[here, first : first + 128] = pair[1] - turn(pair[0], NODES)
            hoops[here, first + 128 : first + 256] = (
                pair[0] + turn(pair[1], NODES) + turn(pair[2], 2 * NODES)
            )
        return 0

    lax.fori_loop(0, HALF // STRIP, strip, 0, unroll=True)

    high, low = parts[:, 0:768], parts[:, 768:1536]
    b_hi, b_lo = block(9)
    straight = dot(high, b_hi) + dot(low, b_hi) + dot(high, b_lo)
    even = straight[:, 0:128] + hoops[:, 0:128]
    odd = straight[:, 128:256] + hoops[:, 256:384]
    half = ANGLES // 2
    for i, value in enumerate((even, hoops[:, 384:512], odd, hoops[:, 128:256])):
        v_hi, v_lo = split(value[0:half])
        sums[half * i : half * i + half, 0:128] = v_hi
        sums[half * i : half * i + half, 128:256] = v_lo

    step = 2.0 * math.pi / ANGLES
    row = lax.broadcasted_iota(jnp.int32, (MODES, 128), 0)
    signed = (0.5 * step) * (1.0 - 2.0 * (row % 2).astype(f32))
    weights = jnp.where(row == 0, 0.5 * signed, signed) * 2.0
    last = jnp.sum(weights * even[0:half], axis=0, keepdims=True) + 0.5 * step * even[half : half + 1]
    pieces = [(sums[half * i : half * i + half, 0:128], sums[half * i : half * i + half, 128:256]) for i in range(4)]
    cos_part = product(*block(2), *pieces[0]) + product(*block(3), *pieces[1])
    result[pl.ds(0, MODES, stride=2), :] = cos_part + signed * even[half : half + 1]
    sin_part = product(*block(4), *pieces[2]) + product(*block(5), *pieces[3])
    sin_part = sin_part + (row.astype(f32) * signed) * hoops[half : half + 1, 128:256]
    result[pl.ds(1, MODES, stride=2), :] = jnp.where(row == 0, last, sin_part)


def kernel(
    disp_in, metric_in, weight_in, radius_in, moduli_in, neigh_in, side_in, pres_in,
    table_in,
    out,
    disp, metric, weights, radii, moduli, neigh, side, pres,
    pack, got1, got2, state1, result, back0, back1, home0, home1, perm, rims, rims_back, rim_out, rim_in, base, traces, partial, final,
    even_odd, turns, grads, parts, hoops, sums,
    table,
    relay1,
    disp_sem, small_sem, table_sem,
    s1, r1, m1, o1, s2, r2, s3, r3, s4, r4, far,
    rim_send, rim_recv,
):
    sems1, sems2, sems3, sems4 = (s1, r1, m1, o1), (s2, r2, None, None), (s3, r3, None, None), (s4, r4, None, None)
    elem = lax.axis_index("elem")
    mode = lax.axis_index("mode")
    runs = lax.axis_size("elem")
    half, rest = mode // 8, mode % 8
    row, core = rest // 2, rest % 2
    height = half * 8 + elem // 4

    def place(dz, dy, dc):
        there = (height + dz + 16) % 16
        column = (row + dy + 4) % 4 * 2 + (core + dc + 2) % 2
        return there % 8 * 4 + elem % 4, there // 8 * 8 + column

    disp_copies = [pltpu.make_async_copy(disp_in.at[s], disp.at[s], disp_sem.at[s]) for s in range(2)]
    for copy in disp_copies:
        copy.start()
    barrier = pltpu.get_barrier_semaphore()
    senders = [place(-LEG * up, -dy, -dc) for dy, dc, up in CROSS] + [place(LEG, 0, 0)]
    senders += [place(0, -dy, -dc) for dy, dc in LOCAL]
    for sender in senders:
        pl.semaphore_signal(barrier, inc=1, device_id=sender, device_id_type=MESH)

    @pl.when(elem > 0)
    def _():
        pl.semaphore_signal(barrier, inc=1, device_id=(elem - 1, mode), device_id_type=MESH)

    @pl.when(elem < runs - 1)
    def _():
        pl.semaphore_signal(barrier, inc=1, device_id=(elem + 1, mode), device_id_type=MESH)

    small_copies = [
        pltpu.make_async_copy(src, dst, small_sem.at[i])
        for i, (src, dst) in enumerate(
            [(metric_in, metric), (weight_in, weights), (radius_in, radii), (moduli_in, moduli),
             (neigh_in, neigh), (side_in, side), (pres_in, pres)]
        )
    ]
    for copy in small_copies:
        copy.start()

    lane = lax.broadcasted_iota(jnp.int32, (OWN, 128), 1)
    lane8 = lax.broadcasted_iota(jnp.int32, (8, 128), 1)

    def column(s, c, g):
        if g < 4:
            return disp[s, c, :, 128 * g : 128 * g + 128]
        return jnp.concatenate([disp[s, c, :, 512:576], jnp.zeros((OWN, 64), f32)], axis=1)

    def gather_element(s, j, base_lane):
        result = jnp.zeros((OWN, 128), f32)
        for c in range(3):
            target = NODES * c + base_lane
            first = NODES * j
            for g in range(first // 128, (first + NODES - 1) // 128 + 1):
                low = max(first, 128 * g)
                high = min(first + NODES, 128 * g + 128)
                moved = turn(column(s, c, g), target - (first - 128 * g))
                begin = (target + low - first) % 128
                end = begin + high - low
                inside = (lane >= begin) & (lane < end)
                if end > 128:
                    inside = (lane >= begin) | (lane < end - 128)
                result = jnp.where(inside, moved, result)
        return result

    def pack_rows(full, ragged):
        last = ragged[24:32]
        tails = [turn(last, 88), turn(last, 48), turn(last, 8)]
        rows = [jnp.where(lane8 < 88, ragged[8 * t : 8 * t + 8], tails[t]) for t in range(3)]
        return jnp.where(lane < 108, full, ragged), jnp.concatenate(rows, axis=0)

    def unpack_ragged(first, second):
        rows = [
            jnp.where(lane8 < 88, second[8 * t : 8 * t + 8], first[8 * t : 8 * t + 8]) for t in range(3)
        ]
        moved = [turn(second[0:8], -88), turn(second[8:16], -48), turn(second[16:24], -8)]
        last = jnp.where(lane8 < 40, moved[0], jnp.where(lane8 < 80, moved[1], moved[2]))
        rows.append(jnp.where(lane8 < 88, last, first[24:32]))
        return jnp.concatenate(rows, axis=0)

    for copy in disp_copies:
        copy.wait()
    for j in range(PEERS):
        full = gather_element(0, j, 0)
        ragged = gather_element(1, j, 108)
        top, bottom = pack_rows(full, ragged)
        pack[j, 0:32, :] = top
        pack[j, 32:56, :] = bottom

    table_copy = pltpu.make_async_copy(table_in, table, table_sem)
    table_copy.start()

    neighbours_there = 2 - (elem == 0).astype(jnp.int32) - (elem == runs - 1).astype(jnp.int32)
    pl.semaphore_wait(barrier, len(senders) + neighbours_there)

    class Exchange:
        def __init__(self, source, target, arrivals, sems, relay=None):
            send, recv, relayed, onward = sems
            self.all = arrivals, relay, send, recv, onward
            self.first, self.second = [], []

            def copy(src, dst, sent, received, to):
                return pltpu.make_async_remote_copy(
                    src_ref=src, dst_ref=dst, send_sem=sent, recv_sem=received,
                    device_id=to, device_id_type=MESH,
                )

            for i, (dy, dc, up) in enumerate(CROSS):
                owner = place(2 * LEG, dy, dc)
                if relay is None:
                    self.first.append(copy(source(owner[1]), target(mode), send, recv, owner))
                    continue
                origin = place(-LEG * up, 0, 0)[1]
                self.first.append(copy(source(owner[1]), relay.at[i], send, relayed.at[i], place(LEG * up, 0, 0)))
                self.second.append(copy(relay.at[i], target(origin), onward, recv, place(LEG * up, dy, dc)))
            for dy, dc in LOCAL:
                to = place(0, dy, dc)
                self.first.append(copy(source(to[1]), target(mode), send, recv, to))

        def start(self):
            for one in self.first:
                one.start()

        def forward(self, low=0, high=8):
            for first, second in zip(self.first[low:high], self.second[low:high]):
                first.wait_recv()
                second.start()

        def arrive(self):
            arrivals, _, _, recv, _ = self.all
            pltpu.make_async_copy(arrivals, arrivals, recv).wait()

        def finish(self):
            arrivals, relay, send, _, onward = self.all
            pltpu.make_async_copy(arrivals, arrivals, send).wait()
            if relay is not None:
                pltpu.make_async_copy(relay, relay, onward).wait()

    def full_rows(me):
        return got1.at[pl.ds(pl.multiple_of(me * OWN, OWN), OWN)]

    there1 = Exchange(lambda to: pack.at[to, 0:32], full_rows, got1.at[0 : 15 * OWN], sems1, relay1)
    there2 = Exchange(lambda to: pack.at[to, 32:56], lambda me: got2.at[me], got2.at[0:15], sems2)
    again0 = Exchange(lambda to: back0.at[to], lambda me: home0.at[me], home0.at[0:15], sems3)
    again1 = Exchange(lambda to: back1.at[to], lambda me: home1.at[me], home1.at[0:15], sems4)
    there1.start()
    for dz in (LEG, -LEG):
        pl.semaphore_signal(far, inc=1, device_id=place(dz, 0, 0), device_id_type=MESH)
    got1[pl.ds(pl.multiple_of(mode * OWN, OWN), OWN), :] = pack[mode, 0:32, :]
    got2[mode] = pack[mode, 32:56, :]

    for copy in small_copies:
        copy.wait()

    def wide(pieces):
        return jnp.concatenate(pieces + [jnp.zeros((1, WIDE - POINTS), f32)], axis=1)

    def as_row(ref):
        return wide([ref[128 * g : min(128 * g + 128, POINTS)].reshape(1, -1) for g in range(5)])

    geo = [wide([metric[i : i + 1, :]]) for i in range(4)] + [as_row(weights), as_row(radii)]
    stacked = jnp.concatenate(geo + [jnp.zeros((2, WIDE), f32)], axis=0)
    stacked = pltpu.roll(stacked, (WIDE - NODES * mode) % WIDE, 1)

    def own_row(i):
        return stacked[i : i + 1, 0:128]

    lane1 = lax.broadcasted_iota(jnp.int32, (1, 128), 1)
    own = [jnp.where(lane1 < NODES, own_row(i), 0.0) for i in range(6)]
    own = [r + turn(r, NODES) for r in own]
    own[5] = jnp.where(lane1 < 2 * NODES, own[5], 1.0)
    shear = moduli[0, mode]
    bulk = moduli[1, mode]

    first_elem = elem * PEERS
    head = jnp.int32(0)
    tail = jnp.int32(0)
    point = lax.broadcasted_iota(jnp.int32, (1, WIDE), 1)
    e_lane = sum((point >= NODES * i).astype(jnp.int32) for i in range(1, PEERS + 1))
    inner = point - NODES * e_lane
    a_lane = sum((inner >= 6 * i).astype(jnp.int32) for i in range(1, 6))
    b_lane = inner - 6 * a_lane
    partner = jnp.full((1, WIDE), -1, jnp.int32)
    sides = jnp.zeros((1, WIDE), jnp.int32)
    for e in range(PEERS):
        prev = neigh[0, e] - first_elem
        nxt = neigh[1, e] - first_elem
        prev_here = (prev >= 0) & (prev < PEERS)
        next_here = (nxt >= 0) & (nxt < PEERS)
        head = head + jnp.where(prev_here, 0, e)
        tail = tail + jnp.where(next_here, 0, e)
        low = jnp.where(prev_here, prev * NODES + 5, -10000)
        high = jnp.where(next_here, nxt * NODES, -10000)
        here = e_lane == e
        partner = jnp.where(here & (b_lane == 0), low + 6 * a_lane, partner)
        partner = jnp.where(here & (b_lane == 5), high + 6 * a_lane, partner)
        sides = jnp.where(here, side[e], sides)
    for g in range(5):
        rows = lax.broadcasted_iota(jnp.int32, (128, WIDE), 0) + 128 * g
        perm[128 * g : 128 * g + 128, :] = jnp.where(rows == partner, 1.0, 0.0).astype(bf16)
    slot = sum((lane1 >= 6 * i).astype(jnp.int32) for i in range(1, 13))
    node = lane1 - 6 * slot
    head_node = jnp.where(slot < 12, head * NODES + 6 * node, -1)
    tail_node = jnp.where(slot < 12, tail * NODES + 6 * node + 5, -1)
    for g in range(5):
        rows = lax.broadcasted_iota(jnp.int32, (128, 128), 0) + 128 * g
        rims[128 * g : 128 * g + 128, 0:128] = jnp.where(rows == head_node, 1.0, 0.0).astype(bf16)
        rims[128 * g : 128 * g + 128, 128:256] = jnp.where(rows == tail_node, 1.0, 0.0).astype(bf16)
    line = lax.broadcasted_iota(jnp.int32, (128, WIDE), 0)
    line_slot = sum((line >= 6 * i).astype(jnp.int32) for i in range(1, 13))
    line_node = 6 * (line - 6 * line_slot)
    line_used = line_slot < 12
    for way, first in ((0, head * NODES), (1, tail * NODES + 5)):
        match = line_used & (point == first + line_node)
        rims_back[128 * way : 128 * way + 128, :] = jnp.where(match, 1.0, 0.0).astype(bf16)
    facing = (a_lane == 5 * sides) & (e_lane < PEERS)
    outward = (2 * sides - 1).astype(f32)
    face = jnp.where(facing, 15.0 * outward * geo[4] * geo[5], 0.0)
    order = lax.broadcasted_iota(jnp.int32, (OWN, 128), 0)
    pressure = jnp.zeros((OWN, 128), f32)
    for i in range(OWN):
        pressure = jnp.where(order == i, pres[i], pressure)
    for g in range(5):
        columns = slice(128 * g, 128 * g + 128)
        base[0, :, columns] = pressure * (face * geo[0])[:, columns]
        base[1, :, columns] = pressure * (face * geo[1])[:, columns]

    table_copy.wait()

    scratch = (even_odd, turns, grads, parts, hoops, sums)

    there1.forward(0, 7)

    @pl.when(half == 0)
    def _():
        pl.semaphore_wait(far, 2)
        there2.start()

    there1.forward(7, 8)

    @pl.when(half == 1)
    def _():
        pl.semaphore_wait(far, 2)
        there2.start()

    there1.arrive()

    evaluate(got1, result, own, shear, bulk, table, scratch)
    for i in range(PEERS):
        block = turn(result[OWN * i : OWN * i + OWN, :], 108)
        _, bottom = pack_rows(block, block)
        back0[i] = bottom
        back1[i] = block
    again0.start()
    home0[mode] = back0[mode]

    there2.arrive()
    for i in range(PEERS):
        state1[OWN * i : OWN * i + OWN, :] = turn(unpack_ragged(got1[OWN * i : OWN * i + OWN, :], got2[i]), 20)

    evaluate(state1, result, own, shear, bulk, table, scratch)
    for i in range(PEERS):
        back1[i] = jnp.where(lane < 108, result[OWN * i : OWN * i + OWN, :], back1[i])
    again1.start()
    home1[mode] = back1[mode]

    def side_by_side(pieces, c):
        columns = []
        for g in range(5):
            acc = jnp.zeros((OWN, 128), f32)
            for i in range(PEERS):
                low = max(NODES * i, 128 * g) - 128 * g
                high = min(NODES * i + NODES, 128 * g + 128) - 128 * g
                if low < high:
                    moved = turn(pieces[i], NODES * i - 128 * g - NODES * c)
                    acc = jnp.where((lane >= low) & (lane < high), moved, acc)
            columns.append(acc)
        whole = jnp.concatenate(columns, axis=1)
        return whole if c == 1 else whole + base[c // 2]

    def assemble(first, l_hi, l_lo, loaded):
        rows = slice(first, first + loaded.shape[0])
        partial[rows, :] = loaded + dot(l_hi, perm[...]) + dot(l_lo, perm[...])

    def trace(first, l_hi, l_lo):
        rows = slice(first, first + l_hi.shape[0])
        traces[rows, :] = dot(l_hi, rims[...]) + dot(l_lo, rims[...])

    again0.arrive()
    early = [turn(unpack_ragged(back1[i], home0[i]), 20) for i in range(PEERS)]
    early = jnp.concatenate([side_by_side(early, 1), side_by_side(early, 2)], axis=0)
    early_parts = split(early)
    trace(0, *early_parts)
    assemble(0, *early_parts, early)
    again1.arrive()
    late = [turn(unpack_ragged(home1[i], home0[i]), 20) for i in range(PEERS)]
    late = [side_by_side(late, 0)] + [side_by_side([home1[i] for i in range(PEERS)], c) for c in range(3)]
    late = jnp.concatenate(late, axis=0)
    late_parts = split(late)
    trace(64, *late_parts)

    for way in range(2):
        columns = slice(128 * way, 128 * way + 128)
        for s in range(2):
            tile = jnp.zeros((8, 128), f32)
            for t in range(12):
                tile = jnp.where(slot == t, traces[96 * s + 8 * t : 96 * s + 8 * t + 8, columns], tile)
            rim_out[way, 8 * s : 8 * s + 8, :] = tile

    to_prev = pltpu.make_async_remote_copy(
        src_ref=rim_out.at[0], dst_ref=rim_in.at[1], send_sem=rim_send.at[0], recv_sem=rim_recv.at[1],
        device_id=(jnp.maximum(elem - 1, 0), mode), device_id_type=MESH,
    )
    to_next = pltpu.make_async_remote_copy(
        src_ref=rim_out.at[1], dst_ref=rim_in.at[0], send_sem=rim_send.at[1], recv_sem=rim_recv.at[0],
        device_id=(jnp.minimum(elem + 1, runs - 1), mode), device_id_type=MESH,
    )

    @pl.when(elem > 0)
    def _():
        to_prev.start()

    @pl.when(elem < runs - 1)
    def _():
        to_next.start()

    assemble(64, *late_parts, late)

    @pl.when(elem > 0)
    def _():
        to_next.wait_recv()

    @pl.when(elem < runs - 1)
    def _():
        to_prev.wait_recv()

    arrived = []
    for way, there in ((0, elem > 0), (1, elem < runs - 1)):
        rows = []
        for s in range(2):
            tile = jnp.where(there, rim_in[way, 8 * s : 8 * s + 8, :], 0.0)
            rows += [jnp.where(slot == t, tile, 0.0) for t in range(12)]
        arrived.append(jnp.concatenate(rows, axis=0))
    a_hi, a_lo = split(jnp.concatenate(arrived, axis=1))
    out_copies = [pltpu.make_async_copy(final.at[s], out.at[s], disp_sem.at[s]) for s in range(2)]
    places = [(0, 1), (0, 2), (0, 0), (1, 0), (1, 1), (1, 2)]
    for s in range(2):
        half_rows = slice(96 * s, 96 * s + 96)
        block = partial[half_rows, :] + dot(a_hi[half_rows], rims_back[...]) + dot(a_lo[half_rows], rims_back[...])
        for i in range(3):
            final[places[3 * s + i]] = block[32 * i : 32 * i + 32, 0:POINTS]
        out_copies[s].start()
    for exchange in (there1, there2, again0, again1):
        exchange.finish()

    @pl.when(elem > 0)
    def _():
        to_prev.wait_send()

    @pl.when(elem < runs - 1)
    def _():
        to_next.wait_send()

    for copy in out_copies:
        copy.wait()


EVALUATE_SCRATCH = [
    pltpu.VMEM((HALF, 256), f32),
    pltpu.VMEM((HALF, 256), f32),
    pltpu.VMEM((HALF, 768), f32),
    pltpu.VMEM((HALF, 1536), bf16),
    pltpu.VMEM((HALF, 512), f32),
    pltpu.VMEM((2 * ANGLES, 256), bf16),
]


def on_device(displacement, metric, weight_jac, radius, moduli, neighbours, inner_side, pressure):
    table = jnp.asarray(tables())
    hbm = pl.BlockSpec(memory_space=pltpu.HBM)
    single = pltpu.SemaphoreType.DMA
    sems = [single, single, pltpu.SemaphoreType.DMA((len(CROSS),)), single] + [single] * 6
    return pl.pallas_call(
        kernel,
        out_shape=jax.ShapeDtypeStruct((2, 3, OWN, POINTS), f32),
        in_specs=[hbm] * 9,
        out_specs=hbm,
        scratch_shapes=[
            pltpu.VMEM((2, 3, OWN, POINTS), f32),
            pltpu.VMEM((4, POINTS), f32),
            pltpu.VMEM((POINTS,), f32),
            pltpu.VMEM((POINTS,), f32),
            pltpu.SMEM((2, PEERS), f32),
            pltpu.SMEM((2, PEERS), jnp.int32),
            pltpu.SMEM((PEERS,), jnp.int32),
            pltpu.SMEM((OWN,), f32),
            pltpu.VMEM((PEERS, 56, 128), f32),
            pltpu.VMEM((COEFS, 128), f32),
            pltpu.VMEM((PEERS, 24, 128), f32),
            pltpu.VMEM((COEFS, 128), f32),
            pltpu.VMEM((COEFS, 128), f32),
            pltpu.VMEM((PEERS, 24, 128), f32),
            pltpu.VMEM((PEERS, 32, 128), f32),
            pltpu.VMEM((PEERS, 24, 128), f32),
            pltpu.VMEM((PEERS, 32, 128), f32),
            pltpu.VMEM((WIDE, WIDE), bf16),
            pltpu.VMEM((WIDE, 256), bf16),
            pltpu.VMEM((256, WIDE), bf16),
            pltpu.VMEM((2, 16, 128), f32),
            pltpu.VMEM((2, 16, 128), f32),
            pltpu.VMEM((2, OWN, WIDE), f32),
            pltpu.VMEM((192, 256), f32),
            pltpu.VMEM((192, WIDE), f32),
            pltpu.VMEM((2, 3, OWN, POINTS), f32),
            *EVALUATE_SCRATCH,
            pltpu.VMEM(table.shape, bf16),
            pltpu.VMEM((len(CROSS), 32, 128), f32),
            pltpu.SemaphoreType.DMA((2,)),
            pltpu.SemaphoreType.DMA((7,)),
            pltpu.SemaphoreType.DMA,
            *sems,
            pltpu.SemaphoreType.REGULAR,
            pltpu.SemaphoreType.DMA((2,)),
            pltpu.SemaphoreType.DMA((2,)),
        ],
        compiler_params=pltpu.CompilerParams(
            collective_id=0, has_side_effects=True, vmem_limit_bytes=64 * 2**20
        ),
        name="bellows",
    )(
        displacement, metric, weight_jac, radius, moduli, neighbours.T, inner_side, pressure,
        table,
    )


def solution(mesh):
    placed = (
        P(None, None, "mode", "elem"),
        P(None, "elem"),
        P("elem"),
        P("elem"),
        P(None, "elem"),
        P("elem", None),
        P("elem"),
        P("mode"),
    )
    return jax.shard_map(
        on_device,
        mesh=mesh,
        in_specs=placed,
        out_specs=P(None, None, "mode", "elem"),
        check_vma=False,
    )
```
